128 devices in a mesh: seq: 16 (over x, y), tp: 8 (over z, core).
Axes of the slice: x: 4, y: 4, z: 4, core: 2. Of those that a mesh axis runs over, the one named last changes fastest.
Arguments:
- hidden: bfloat16 [2048, 5120], P(('seq', 'tp')), may hold values from -6 to 6
- query_weight: bfloat16 [5120, 8192], P(None, 'tp'), may hold values from -0.078125 to 0.078125
- key_weight: bfloat16 [5120, 1024], P(None, 'tp'), may hold values from -0.078125 to 0.078125
- value_weight: bfloat16 [5120, 1024], P(None, 'tp'), may hold values from -0.078125 to 0.078125
- prefix_cache: bfloat16 [32768, 8, 2, 128], P('seq', 'tp'), may hold values from -10.4 to 10.4
- owner_prompt: int32 [16], P('seq'), may hold values from 0 to 3, as said below
- response_length: int32 [64], P('seq'), may hold values from 1 to 32
- context_grad: bfloat16 [2048, 8192], P('seq', 'tp'), may hold values from -6 to 6
Outputs:
- context: bfloat16 [2048, 8192], P('seq', 'tp')
- hidden_grad: bfloat16 [2048, 5120], P(('seq', 'tp'))
- prefix_grad: bfloat16 [32768, 8, 2, 128], P('seq', 'tp')
The draws below stay inside these ranges and needn't reach their ends.
Inputs may be any that keep to these rules, and one draw needn't show every extreme that they name: `owner_prompt`: each prompt index appears exactly 16 / 4 times.
All inputs are finite; a program needn't handle non-finite values.
Results may differ from the reference program's by a relative error of at most 0.024.
Values may be sent and summed in bfloat16 or wider, within the bound.
No kernel may reach another device: no remote copies, remote signals or barrier semaphores. Data moves between devices by JAX's collectives and lax.ppermute only.
A program may use at most 192 MiB of HBM per device.

```python
import jax
import jax.numpy as jnp
from jax import lax

D = 5120
QH = 64
KVH = 8
HD = 128
PREFIX = 8192
FAN = 16
RESP_DEV = 4
RESP_LEN = 32
OWNERS = 16
RESPONSES = 64
PROMPTS = 4
RROWS = 2048
PTOKENS = 32768


def draw_owner_prompt(key, part):
    key = jax.random.fold_in(key, 11)
    shuffled = jax.random.permutation(key, jnp.arange(OWNERS, dtype=jnp.int32))
    return (shuffled // (FAN // RESP_DEV)).astype(jnp.int32)


def draw_response_length(key, part):
    key = jax.random.fold_in(key, 23)
    first_key, second_key = jax.random.split(key)
    lengths = jax.random.randint(first_key, (RESPONSES,), 1, RESP_LEN + 1, dtype=jnp.int32)
    shuffled = jax.random.permutation(second_key, jnp.arange(RESPONSES, dtype=jnp.int32))
    indices = jnp.arange(RESPONSES, dtype=jnp.int32)
    lengths = jnp.where(indices == shuffled[0], RESP_LEN, lengths)
    lengths = jnp.where(indices == shuffled[1], 1, lengths)
    return lengths.astype(jnp.int32)


def draw_prefix_cache(key, part):
    key = jax.random.fold_in(key, 37)
    base_key = jax.random.fold_in(key, 0)
    base_values = jax.random.truncated_normal(base_key, -4.0, 4.0, (PTOKENS, KVH, 2, HD), jnp.float32)
    levels = jnp.ones((KVH,), jnp.float32)
    factor = jnp.stack([levels, jnp.ones((KVH,), jnp.float32)], axis=1)
    return (base_values * factor[None, :, :, None]).astype(jnp.bfloat16)


def level_of(stream_key, shape, shards, smallest, top_value):
    level, own = 1.0, jax.random.fold_in(stream_key, 6)
    for axis_at, parts in shards:
        heights = jnp.exp(jax.random.uniform(jax.random.fold_in(own, axis_at), (parts,), jnp.float32, smallest / len(shards), top_value / len(shards)))
        level = level * jnp.repeat(heights, shape[axis_at] // parts).reshape([-1 if axis == axis_at else 1 for axis in range(len(shape))])
    return level


def centred(stream_key, dims, spread, bound, cuts=(), kind=jnp.bfloat16):
    gain = level_of(stream_key, dims, cuts, -0.22, 0.18) if cuts else 1.0
    values = jax.random.normal(stream_key, dims, jnp.float32) * spread * gain
    return jnp.minimum(jnp.maximum(values, -bound), bound).astype(kind)


def setup_inputs(seed: int = 0) -> dict:
    seeds = jax.random.split(jax.random.key(seed), 9)
    return {
        "hidden": centred(seeds[0], (RROWS, D), 1.0, 6.0, ((0, 128),)),
        "query_weight": centred(seeds[1], (D, QH * HD), D ** -0.5, 0.078125, ((1, 8),)),
        "key_weight": centred(seeds[2], (D, KVH * HD), D ** -0.5, 0.078125, ((1, 8),)),
        "value_weight": centred(seeds[3], (D, KVH * HD), D ** -0.5, 0.078125, ((1, 8),)),
        "prefix_cache": draw_prefix_cache(jax.random.fold_in(seeds[8], 71), 0),
        "owner_prompt": draw_owner_prompt(jax.random.fold_in(seeds[8], 71), 0),
        "response_length": draw_response_length(jax.random.fold_in(seeds[8], 71), 0),
        "context_grad": centred(seeds[7], (RROWS, QH * HD), 1.0, 6.0, ((0, 16), (1, 8))),
    }


big_negative = -1.0e30


def reference(hidden, query_weight, key_weight, value_weight, prefix_cache, owner_prompt, response_length, context_grad):
    score_scale = HD ** -0.5
    query_group = QH // KVH
    queries = jnp.dot(hidden, query_weight, preferred_element_type=jnp.float32).astype(jnp.bfloat16)
    resp_keys = jnp.dot(hidden, key_weight, preferred_element_type=jnp.float32).astype(jnp.bfloat16)
    resp_values = jnp.dot(hidden, value_weight, preferred_element_type=jnp.float32).astype(jnp.bfloat16)
    query_shape = (OWNERS, RESP_DEV, RESP_LEN, KVH, query_group, HD)
    pair_shape = (OWNERS, RESP_DEV, RESP_LEN, KVH, HD)
    prompt_cache = prefix_cache.reshape(PROMPTS, PREFIX, KVH, 2, HD)
    position = jnp.arange(RESP_LEN, dtype=jnp.int32)
    causal = position[None, :] <= position[:, None]
    prefix_open = jnp.ones((RESP_LEN, PREFIX), dtype=bool)

    def one_response(query_rows, own_keys, own_values, grad_raw, length, cached):
        live_rows = position < length
        usable = jnp.concatenate([prefix_open, causal & live_rows[None, :]], axis=1)
        all_keys = jnp.concatenate([cached[:, :, 0], own_keys], axis=0).astype(jnp.float32)
        all_values = jnp.concatenate([cached[:, :, 1], own_values], axis=0).astype(jnp.float32)
        query_float = query_rows.astype(jnp.float32)
        scores = jnp.einsum("tgjd,sgd->gjts", query_float, all_keys) * score_scale
        scores = jnp.where(usable, scores, big_negative)
        row_max = jnp.max(scores, axis=-1)
        unnormed = jnp.where(usable, jnp.exp(scores - row_max[..., None]), 0.0)
        row_sum = jnp.sum(unnormed, axis=-1)
        rounded = lax.optimization_barrier(unnormed.astype(jnp.bfloat16)).astype(jnp.float32)
        weighted = jnp.einsum("gjts,sgd->tgjd", rounded, all_values)
        context = weighted / jnp.transpose(row_sum, (2, 0, 1))[..., None]
        context = jnp.where(live_rows[:, None, None, None], context, 0.0).astype(jnp.bfloat16)
        log_norm = row_max + jnp.log(row_sum)
        out_grad = jnp.where(live_rows[:, None, None, None], grad_raw, jnp.zeros_like(grad_raw)).astype(jnp.float32)
        correction = jnp.sum(out_grad * context.astype(jnp.float32), axis=-1)
        attention = jnp.where(usable, jnp.exp(scores - log_norm[..., None]), 0.0)
        weight_grad = jnp.einsum("tgjd,sgd->gjts", out_grad, all_values)
        score_grad = attention * (weight_grad - jnp.transpose(correction, (1, 2, 0))[..., None])
        grad_round = lax.optimization_barrier(score_grad.astype(jnp.bfloat16)).astype(jnp.float32)
        attention_round = lax.optimization_barrier(attention.astype(jnp.bfloat16)).astype(jnp.float32)
        query_grad = jnp.einsum("gjts,sgd->tgjd", grad_round, all_keys) * score_scale
        key_grad = jnp.einsum("gjts,tgjd->sgd", grad_round, query_float) * score_scale
        value_grad = jnp.einsum("gjts,tgjd->sgd", attention_round, out_grad)
        return context, query_grad, key_grad, value_grad

    def owner_step(totals, inputs):
        query_dev, keys_dev, values_dev, grads_dev, lengths_dev, prompt = inputs
        cached = lax.dynamic_index_in_dim(prompt_cache, prompt, 0, keepdims=False)
        partial_sum = jnp.zeros((PREFIX, KVH, 2, HD), jnp.float32)
        contexts, query_grads, key_grads, value_grads = [], [], [], []
        for member in range(RESP_DEV):
            context, query_grad, key_grad, value_grad = one_response(
                query_dev[member], keys_dev[member], values_dev[member], grads_dev[member], lengths_dev[member], cached)
            partial_sum = partial_sum + jnp.stack([key_grad[:PREFIX], value_grad[:PREFIX]], axis=2)
            contexts.append(context)
            query_grads.append(query_grad.astype(jnp.bfloat16))
            key_grads.append(key_grad[PREFIX:].astype(jnp.bfloat16))
            value_grads.append(value_grad[PREFIX:].astype(jnp.bfloat16))
        rounded = lax.optimization_barrier(partial_sum.astype(jnp.bfloat16)).astype(jnp.float32)
        current = lax.dynamic_index_in_dim(totals, prompt, 0, keepdims=False)
        totals = lax.dynamic_update_index_in_dim(totals, current + rounded, prompt, 0)
        return totals, (jnp.stack(contexts), jnp.stack(query_grads), jnp.stack(key_grads), jnp.stack(value_grads))

    totals = jnp.zeros((PROMPTS, PREFIX, KVH, 2, HD), jnp.float32)
    scanned = (queries.reshape(query_shape), resp_keys.reshape(pair_shape), resp_values.reshape(pair_shape),
               context_grad.reshape(query_shape), response_length.reshape(OWNERS, RESP_DEV), owner_prompt)
    totals, stacked = lax.scan(owner_step, totals, scanned)
    contexts, query_grads, key_grads, value_grads = stacked
    context = contexts.reshape(RROWS, QH * HD)
    query_grad = query_grads.reshape(RROWS, QH * HD)
    key_grad = key_grads.reshape(RROWS, KVH * HD)
    value_grad = value_grads.reshape(RROWS, KVH * HD)
    hidden_grad = (jnp.dot(query_grad, query_weight.T, preferred_element_type=jnp.float32)
                   + jnp.dot(key_grad, key_weight.T, preferred_element_type=jnp.float32)
                   + jnp.dot(value_grad, value_weight.T, preferred_element_type=jnp.float32)).astype(jnp.bfloat16)
    prefix_grad = totals.reshape(PTOKENS, KVH, 2, HD).astype(jnp.bfloat16)
    return context, hidden_grad, prefix_grad
```

```python
import functools
import math

import jax
import jax.numpy as jnp
from jax import lax
from jax.experimental import pallas as pl
from jax.experimental.pallas import tpu as pltpu
from jax.sharding import PartitionSpec as P

HD = 128
RESP_LEN = 32
ROWS = 128
SLICE = 256
STAT_ROWS = 16
CHUNK = 2048
HALF = 1024
KEYS = 8192
WROWS = 1024
BLOCK = 1024
SCALE = HD ** -0.5
EXP2_SCALE = SCALE * math.log2(math.e)
NEG = -1.0e30
BF = jnp.bfloat16
F32 = jnp.float32
NT = (((1,), (1,)), ((), ()))
NN = (((1,), (0,)), ((), ()))
ANY = pl.BlockSpec(memory_space=pl.ANY)
VM = pl.BlockSpec(memory_space=pltpu.VMEM)
XG = [[a * 4 + b for a in range(4)] for b in range(4)]


def dot(a, b, dims):
    return lax.dot_general(a, b, dims, preferred_element_type=F32)


def move_tp(x, dz, dc):
    pairs = [(z * 2 + c, ((z + dz) % 4) * 2 + (c + dc) % 2) for z in range(4) for c in range(2)]
    return lax.ppermute(x, "tp", pairs)


def move_seq(x, dx, dy):
    pairs = [(a * 4 + b, ((a + dx) % 4) * 4 + (b + dy) % 4) for a in range(4) for b in range(4)]
    return lax.ppermute(x, "seq", pairs)


def ring_gather(a, b, move):
    pa, pb = move(a, 1), move(b, 1)
    nb, na = move(b, -1), move(a, -1)
    return [a, b, pa, pb, na, nb, move(pa, 1), move(nb, -1)]


def split3(v):
    hi = v.astype(BF).astype(F32)
    mid = (v - hi).astype(BF).astype(F32)
    return hi, mid, v - hi - mid


def stat_rows(first, second):
    rows = list(split3(first)) + list(split3(second))
    return jnp.concatenate(rows + [jnp.zeros((STAT_ROWS - 6, SLICE), F32)], axis=0).astype(BF)


def read_stats(rows):
    r = rows.astype(F32)
    return r[0:1] + r[1:2] + r[2:3], r[3:4] + r[4:5] + r[5:6]


def causal_mask(lens):
    key = lax.broadcasted_iota(jnp.int32, (ROWS, ROWS), 0)
    row = lax.broadcasted_iota(jnp.int32, (ROWS, ROWS), 1)
    member = lax.shift_right_logical(key, 5)
    length = jnp.where(member == 0, lens[0], jnp.where(member == 1, lens[1], jnp.where(member == 2, lens[2], lens[3])))
    live = (key & (RESP_LEN - 1)) < length
    return (member == lax.shift_right_logical(row, 5)) & (key <= row) & live


def grads_kernel(meta, cg_ref, out_ref):
    pos = lax.broadcasted_iota(jnp.int32, (ROWS, SLICE), 0)
    member = lax.shift_right_logical(pos, 5)
    length = jnp.where(member == 0, meta[4], jnp.where(member == 1, meta[5], jnp.where(member == 2, meta[6], meta[7])))
    live = (pos & (RESP_LEN - 1)) < length
    out_ref[0] = jnp.where(live, cg_ref[...], jnp.zeros_like(cg_ref))


def masked_grads(meta, context_grad):
    return pl.pallas_call(
        grads_kernel,
        grid_spec=pltpu.PrefetchScalarGridSpec(
            num_scalar_prefetch=1,
            grid=(4,),
            in_specs=[pl.BlockSpec((ROWS, SLICE), lambda i, m: (0, (m[1] + i) % 4))],
            out_specs=pl.BlockSpec((1, ROWS, SLICE), lambda i, m: (i, 0, 0)),
        ),
        out_shape=jax.ShapeDtypeStruct((4, ROWS, SLICE), BF),
        name="masked_grads",
    )(meta, context_grad)


def project_kernel(meta, *refs):
    pieces, (wq, wk, wv, og), (out, k_out, v_out), (seg, sem) = refs[:10], refs[10:14], refs[14:17], refs[17:]
    i = pl.program_id(0)

    @pl.when(i == 0)
    def _():
        z, c = meta[2], meta[3]
        half = seg.shape[1] // 2
        copies = []
        for rc in range(2):
            mine = pieces[rc * 5:rc * 5 + 5]
            for n, (dz, col, width) in enumerate(((0, 0, 2 * half), (3, 0, 2 * half), (1, 0, 2 * half), (2, 0, half), (2, half, half))):
                start = pl.multiple_of((((z + dz) & 3) * 2 + (c ^ rc)) * 16, 16)
                copies.append(pltpu.make_async_copy(mine[n], seg.at[pl.ds(start, 16), pl.ds(col, width)], sem.at[rc * 5 + n]))
        for copy in copies:
            copy.start()
        for copy in copies:
            copy.wait()
        k_out[...] = dot(seg[...], wk[...], NN).astype(BF)
        v_out[...] = dot(seg[...], wv[...], NN).astype(BF)

    q = dot(seg[...], wq[...], NN).astype(BF)
    out[0, :ROWS] = q
    mask = causal_mask([meta[4], meta[5], meta[6], meta[7]])
    lses, corrs = [], []
    for j in range(2):
        cols = slice(j * HD, (j + 1) * HD)
        s = jnp.where(mask, dot(k_out[...], q[:, cols], NT) * SCALE, NEG)
        top = jnp.max(s, axis=0, keepdims=True)
        p = jnp.where(mask, jnp.exp(s - top), 0.0)
        total = jnp.sum(p, axis=0, keepdims=True)
        dp = dot(v_out[...], og[0, :, cols], NT)
        lses.append(top + jnp.log(total))
        corrs.append(jnp.sum(p.astype(BF).astype(F32) * dp, axis=0, keepdims=True) / total)
    out[0, ROWS:] = stat_rows(jnp.concatenate(lses, axis=1), jnp.concatenate(corrs, axis=1))


def project(meta, pieces, wq, wk, wv, og_rel):
    d = wq.shape[0]
    return pl.pallas_call(
        project_kernel,
        grid_spec=pltpu.PrefetchScalarGridSpec(
            num_scalar_prefetch=1,
            grid=(4,),
            in_specs=[ANY] * 10 + [
                pl.BlockSpec((d, SLICE), lambda i, m: (0, (m[1] + i) % 4)),
                pl.BlockSpec((d, HD), lambda i, m: (0, 0)),
                pl.BlockSpec((d, HD), lambda i, m: (0, 0)),
                pl.BlockSpec((1, ROWS, SLICE), lambda i, m: (i, 0, 0)),
            ],
            out_specs=[
                pl.BlockSpec((1, ROWS + STAT_ROWS, SLICE), lambda i, m: (i, 0, 0)),
                pl.BlockSpec((ROWS, HD), lambda i, m: (0, 0)),
                pl.BlockSpec((ROWS, HD), lambda i, m: (0, 0)),
            ],
            scratch_shapes=[pltpu.VMEM((ROWS, d), BF), pltpu.SemaphoreType.DMA((10,))],
        ),
        out_shape=[
            jax.ShapeDtypeStruct((4, ROWS + STAT_ROWS, SLICE), BF),
            jax.ShapeDtypeStruct((ROWS, HD), BF),
            jax.ShapeDtypeStruct((ROWS, HD), BF),
        ],
        compiler_params=pltpu.CompilerParams(vmem_limit_bytes=24 << 20),
        cost_estimate=pl.CostEstimate(flops=2 * ROWS * d * 1280, bytes_accessed=d * 1280 * 2, transcendentals=0),
        name="project",
    )(meta, *pieces, wq, wk, wv, og_rel)


def worker_kernel(meta, *refs):
    q_in, og_in, kv_in = refs[:8], refs[8:16], refs[16:24]
    dq_out, ctx_out, q_all, og_all, a_hbm, ds_hbm = refs[24:30]
    qslot, ogslot, kv, p_all, ds_all, acc, dqt, mblk, m_ref, l_ref, sem_in, sem_kv, sem_out = refs[30:]
    blocks = KEYS // BLOCK

    kv_copies = [pltpu.make_async_copy(kv_in[n], kv.at[pl.ds(n * HALF, HALF)], sem_kv.at[n]) for n in range(8)]
    for r in range(4):
        code, place = meta[8 + r], meta[12 + r]
        for n in range(8):
            @pl.when(code == n)
            def _():
                pltpu.make_async_copy(q_in[n].at[place], qslot.at[r], sem_in.at[r]).start()
                pltpu.make_async_copy(og_in[n].at[place], ogslot.at[r], sem_in.at[4 + r]).start()
    for copy in kv_copies:
        copy.start()
    dq_out[...] = jnp.zeros_like(dq_out)
    ctx_out[...] = jnp.zeros_like(ctx_out)
    m_ref[...] = jnp.full_like(m_ref, NEG)
    l_ref[...] = jnp.zeros_like(l_ref)
    acc[...] = jnp.zeros_like(acc)
    dqt[...] = jnp.zeros_like(dqt)
    for r in range(4):
        pltpu.make_async_copy(q_in[0].at[0], qslot.at[r], sem_in.at[r]).wait()
        pltpu.make_async_copy(og_in[0].at[0], ogslot.at[r], sem_in.at[4 + r]).wait()
        for j in range(2):
            rows = slice(r * SLICE + j * HD, r * SLICE + (j + 1) * HD)
            cols = slice(j * HD, (j + 1) * HD)
            q_all[rows] = qslot[r, :ROWS, cols]
            og_all[rows] = ogslot[r, :, cols]
    for copy in kv_copies:
        copy.wait()

    def forward(b, _):
        keys = pl.ds(pl.multiple_of(b * BLOCK, BLOCK), BLOCK)
        kb = kv[keys, :HD]
        vt = kv[keys, HD:].T
        for r in range(4):
            rs = slice(r * SLICE, (r + 1) * SLICE)
            s = dot(kb, q_all[rs], NT)
            old = m_ref[:, rs]
            new = jnp.maximum(old, jnp.max(s, axis=0, keepdims=True))
            p = jnp.exp2((s - new) * EXP2_SCALE)
            factor = jnp.exp2((old - new) * EXP2_SCALE)
            l_ref[:, rs] = l_ref[:, rs] * factor + jnp.sum(p, axis=0, keepdims=True)
            pb = p.astype(BF)
            p_all[keys, rs] = pb
            acc[:, rs] = acc[:, rs] * factor + dot(vt, pb, NN)
            m_ref[:, rs] = new
            mblk[pl.ds(b, 1), rs] = new
        return 0

    lax.fori_loop(0, blocks, forward, 0)

    norms, corrs = [], []
    for r in range(4):
        rs = slice(r * SLICE, (r + 1) * SLICE)
        lse0, corr0 = read_stats(qslot[r, ROWS:])
        lse = m_ref[:, rs] * SCALE + jnp.log(l_ref[:, rs])
        top = jnp.maximum(lse, lse0)
        log_norm = top + jnp.log(jnp.exp(lse - top) + jnp.exp(lse0 - top))
        inv = jnp.exp(lse - log_norm) / l_ref[:, rs]
        ctx = acc[:, rs] * inv
        ogt = og_all[rs].astype(F32).T
        corr = jnp.sum(ogt * ctx, axis=0, keepdims=True) + corr0 * jnp.exp(lse0 - log_norm)
        ctx_rows = ctx.T
        spot = meta[16 + r]
        for j in range(2):
            ctx_out[spot, :, j * HD:(j + 1) * HD] = ctx_rows[j * HD:(j + 1) * HD].astype(BF)
        dq_out[spot, ROWS:] = stat_rows(log_norm, corr)
        norms.append(inv)
        corrs.append(corr)

    def backward(b, _):
        keys = pl.ds(pl.multiple_of(b * BLOCK, BLOCK), BLOCK)
        kt = kv[keys, :HD].T
        vb = kv[keys, HD:]
        for r in range(4):
            rs = slice(r * SLICE, (r + 1) * SLICE)
            dp = dot(vb, og_all[rs], NT)
            factor = jnp.exp2((mblk[pl.ds(b, 1), rs] - m_ref[:, rs]) * EXP2_SCALE) * norms[r]
            a = p_all[keys, rs].astype(F32) * factor
            ds = (a * (dp - corrs[r])).astype(BF)
            p_all[keys, rs] = a.astype(BF)
            ds_all[keys, rs] = ds
            dqt[:, rs] += dot(kt, ds, NN)
        pltpu.make_async_copy(p_all.at[keys], a_hbm.at[keys], sem_out.at[0, b]).start()
        pltpu.make_async_copy(ds_all.at[keys], ds_hbm.at[keys], sem_out.at[1, b]).start()
        return 0

    lax.fori_loop(0, blocks, backward, 0)
    for r in range(4):
        rows = (dqt[:, r * SLICE:(r + 1) * SLICE] * SCALE).T
        for j in range(2):
            dq_out[meta[16 + r], :ROWS, j * HD:(j + 1) * HD] = rows[j * HD:(j + 1) * HD].astype(BF)
    for b in range(blocks):
        keys = pl.ds(b * BLOCK, BLOCK)
        pltpu.make_async_copy(p_all.at[keys], a_hbm.at[keys], sem_out.at[0, b]).wait()
        pltpu.make_async_copy(ds_all.at[keys], ds_hbm.at[keys], sem_out.at[1, b]).wait()


def work(meta, q_parts, og_parts, kv_parts):
    blocks = KEYS // BLOCK
    return pl.pallas_call(
        worker_kernel,
        in_specs=[pl.BlockSpec(memory_space=pltpu.SMEM)] + [ANY] * 24,
        out_specs=[VM, VM, VM, VM, ANY, ANY],
        out_shape=[
            jax.ShapeDtypeStruct((16, ROWS + STAT_ROWS, SLICE), BF),
            jax.ShapeDtypeStruct((16, ROWS, SLICE), BF),
            jax.ShapeDtypeStruct((WROWS, HD), BF),
            jax.ShapeDtypeStruct((WROWS, HD), BF),
            jax.ShapeDtypeStruct((KEYS, WROWS), BF),
            jax.ShapeDtypeStruct((KEYS, WROWS), BF),
        ],
        scratch_shapes=[
            pltpu.VMEM((4, ROWS + STAT_ROWS, SLICE), BF),
            pltpu.VMEM((4, ROWS, SLICE), BF),
            pltpu.VMEM((KEYS, SLICE), BF),
            pltpu.VMEM((KEYS, WROWS), BF),
            pltpu.VMEM((KEYS, WROWS), BF),
            pltpu.VMEM((HD, WROWS), F32),
            pltpu.VMEM((HD, WROWS), F32),
            pltpu.VMEM((blocks, WROWS), F32),
            pltpu.VMEM((1, WROWS), F32),
            pltpu.VMEM((1, WROWS), F32),
            pltpu.SemaphoreType.DMA((8,)),
            pltpu.SemaphoreType.DMA((8,)),
            pltpu.SemaphoreType.DMA((2, blocks)),
        ],
        compiler_params=pltpu.CompilerParams(vmem_limit_bytes=58 << 20),
        cost_estimate=pl.CostEstimate(flops=8 * WROWS * KEYS * HD, bytes_accessed=40 << 20, transcendentals=WROWS * KEYS),
        name="attention",
    )(meta, *q_parts, *og_parts, *kv_parts)


def cache_grad_kernel(a_ref, ds_ref, q_ref, og_ref, out_a, out_b):
    dk = dot(ds_ref[...], q_ref[...], NN) * SCALE
    dv = dot(a_ref[...], og_ref[...], NN)
    both = jnp.concatenate([dk, dv], axis=1).astype(BF)
    i = pl.program_id(0)

    @pl.when(i < 2)
    def _():
        out_a[...] = both

    @pl.when(i >= 2)
    def _():
        out_b[...] = both


def cache_grad(chunk, a, ds, q_all, og_all):
    size = CHUNK // 4
    return pl.pallas_call(
        cache_grad_kernel,
        grid=(4,),
        in_specs=[
            pl.BlockSpec((size, WROWS), lambda i: (chunk * 4 + i, 0)),
            pl.BlockSpec((size, WROWS), lambda i: (chunk * 4 + i, 0)),
            pl.BlockSpec((WROWS, HD), lambda i: (0, 0)),
            pl.BlockSpec((WROWS, HD), lambda i: (0, 0)),
        ],
        out_specs=[
            pl.BlockSpec((size, SLICE), lambda i: (jnp.minimum(i, 1), 0)),
            pl.BlockSpec((size, SLICE), lambda i: (jnp.maximum(i - 2, 0), 0)),
        ],
        out_shape=[jax.ShapeDtypeStruct((HALF, SLICE), BF)] * 2,
        compiler_params=pltpu.CompilerParams(vmem_limit_bytes=24 << 20),
        cost_estimate=pl.CostEstimate(flops=4 * CHUNK * WROWS * HD, bytes_accessed=9 << 20, transcendentals=0),
        name="cache_grad",
    )(a, ds, q_all, og_all)


def hidden_kernel(meta, *refs):
    dq_in, (qs, og, k, v, wq, wk, wv), (out,), (dq_s, dk_s, dv_s, part) = refs[:4], refs[4:11], refs[11:12], refs[12:]
    i = pl.program_id(0)

    @pl.when(i == 0)
    def _():
        mask = causal_mask([meta[4], meta[5], meta[6], meta[7]])
        dk = jnp.zeros((ROWS, HD), F32)
        dv = jnp.zeros((ROWS, HD), F32)
        for n in range(4):
            rel = (4 - n) % 4
            log_norm, corr = read_stats(dq_in[n][ROWS:])
            start = pl.multiple_of(((meta[1] + rel) & 3) * SLICE, SLICE)
            for j in range(2):
                cols = slice(j * HD, (j + 1) * HD)
                qj, ogj = qs[rel, :ROWS, cols], og[rel, :, cols]
                s = dot(k[...], qj, NT) * SCALE
                a = jnp.where(mask, jnp.exp(jnp.where(mask, s - log_norm[:, cols], 0.0)), 0.0)
                ds = (a * (dot(v[...], ogj, NT) - corr[:, cols]))
                dsb = ds.astype(BF)
                dk += dot(dsb, qj, NN)
                dv += dot(a.astype(BF), ogj, NN)
                dq = dot(ds.T.astype(BF), k[...], NN) * SCALE
                dq_s[:, pl.ds(start + j * HD, HD)] = (dq_in[n][:ROWS, cols].astype(F32) + dq).astype(BF)
        dk_s[...] = (dk * SCALE).astype(BF)
        dv_s[...] = dv.astype(BF)

    part[...] = dot(dq_s[...], wq[...], NT) + dot(dk_s[...], wk[...], NT) + dot(dv_s[...], wv[...], NT)
    z, c = meta[2], meta[3]
    for rc in range(2):
        for dz in range(4):
            start = pl.multiple_of((((z + dz) & 3) * 2 + (c ^ rc)) * 16, 16)
            out[rc, dz] = part[pl.ds(start, 16), :].astype(BF)


def hidden_grad_parts(meta, dq_parts, q_rel, og_rel, k, v, wq, wk, wv):
    d = wq.shape[0]
    size = 512
    full = lambda shape: pl.BlockSpec(shape, lambda i, m: (0,) * len(shape))
    return pl.pallas_call(
        hidden_kernel,
        grid_spec=pltpu.PrefetchScalarGridSpec(
            num_scalar_prefetch=1,
            grid=(d // size,),
            in_specs=[full((ROWS + STAT_ROWS, SLICE))] * 4 + [
                full((4, ROWS + STAT_ROWS, SLICE)),
                full((4, ROWS, SLICE)),
                full((ROWS, HD)),
                full((ROWS, HD)),
                pl.BlockSpec((size, 1024), lambda i, m: (i, 0)),
                pl.BlockSpec((size, HD), lambda i, m: (i, 0)),
                pl.BlockSpec((size, HD), lambda i, m: (i, 0)),
            ],
            out_specs=pl.BlockSpec((2, 4, 16, size), lambda i, m: (0, 0, 0, i)),
            scratch_shapes=[
                pltpu.VMEM((ROWS, 1024), BF),
                pltpu.VMEM((ROWS, HD), BF),
                pltpu.VMEM((ROWS, HD), BF),
                pltpu.VMEM((ROWS, size), F32),
            ],
        ),
        out_shape=jax.ShapeDtypeStruct((2, 4, 16, d), BF),
        compiler_params=pltpu.CompilerParams(vmem_limit_bytes=24 << 20),
        cost_estimate=pl.CostEstimate(flops=2 * ROWS * d * 1280, bytes_accessed=d * 1280 * 2, transcendentals=0),
        name="hidden_grad",
    )(meta, *dq_parts, q_rel, og_rel, k, v, wq, wk, wv)


def context_kernel(meta, *refs):
    ctx_in, (qs, k, v, dq0, dq1, dq2, dq3), (out,) = refs[:4], refs[4:11], refs[11:]
    stats = (dq0, dq1, dq2, dq3)
    mask = causal_mask([meta[4], meta[5], meta[6], meta[7]])
    row = lax.broadcasted_iota(jnp.int32, (ROWS, HD), 0)
    member = lax.shift_right_logical(row, 5)
    length = jnp.where(member == 0, meta[4], jnp.where(member == 1, meta[5], jnp.where(member == 2, meta[6], meta[7])))
    live = (row & (RESP_LEN - 1)) < length
    for n in range(4):
        rel = (4 - n) % 4
        log_norm, _ = read_stats(stats[n][ROWS:])
        start = pl.multiple_of(((meta[1] + rel) & 3) * SLICE, SLICE)
        for j in range(2):
            cols = slice(j * HD, (j + 1) * HD)
            s = dot(k[...], qs[rel, :ROWS, cols], NT) * SCALE
            a = jnp.where(mask, jnp.exp(jnp.where(mask, s - log_norm[:, cols], 0.0)), 0.0)
            own = dot(a.T.astype(BF), v[...], NN)
            total = jnp.where(live, ctx_in[n][:, cols].astype(F32) + own, 0.0)
            out[:, pl.ds(start + j * HD, HD)] = total.astype(BF)


def finish_context(meta, ctx_parts, q_rel, k, v, dq_parts):
    return pl.pallas_call(
        context_kernel,
        in_specs=[pl.BlockSpec(memory_space=pltpu.SMEM)] + [VM] * 11,
        out_specs=VM,
        out_shape=jax.ShapeDtypeStruct((ROWS, 1024), BF),
        compiler_params=pltpu.CompilerParams(vmem_limit_bytes=16 << 20),
        name="context",
    )(meta, *ctx_parts, q_rel, k, v, *dq_parts)


def send_back(dense):
    shape = dense.shape
    mine = lax.psum_scatter(dense.reshape(-1, SLICE), "seq", scatter_dimension=0, tiled=True, axis_index_groups=XG)
    mine = mine.reshape(4, shape[1], SLICE)
    return [mine[0]] + [move_seq(mine[n], 0, n) for n in (1, 2, 3)]


def spread(parts):
    here = [parts[0]] + [move_seq(parts[n], 0, n) for n in (1, 2, 3)]
    a = jnp.stack([here[0], here[1]])
    b = jnp.stack([here[2], here[3]])
    return ring_gather(a, b, lambda v, d: move_seq(v, d, 0))


def on_device(hidden, wq, wk, wv, prefix_cache, owner_prompt, response_length, context_grad):
    seq, tp = lax.axis_index("seq"), lax.axis_index("tp")
    x, y, z, c = seq // 4, seq % 4, tp // 2, tp % 2
    place = jnp.stack([x, y, z, c]).astype(jnp.int32)
    base = jnp.concatenate([place, response_length])

    prompts = lax.all_gather(owner_prompt, "seq", axis=0, tiled=True)
    owners = jnp.arange(16, dtype=jnp.int32)
    match = prompts == x
    rank = jnp.sum(match[None, :] & (owners[None, :] < owners[:, None]), axis=1)
    chosen = match[None, :] & (rank[None, :] == jnp.arange(4)[:, None])
    sel = jnp.sum(jnp.where(chosen, owners[None, :], 0), axis=1).astype(jnp.int32)
    sel_x, sel_y = sel // 4, sel % 4
    dx, dy = (x - sel_x) % 4, (y - sel_y) % 4
    ring_at = jnp.where(dx == 0, 0, jnp.where(dx == 1, 1, jnp.where(dx == 3, 2, 3)))
    code = ring_at * 2 + dy // 2
    spot = sel_x * 4 + (sel_y - y) % 4
    meta = jnp.concatenate([base, code, dy % 2, spot]).astype(jnp.int32)

    cache = prefix_cache.reshape(CHUNK, SLICE)
    kv_parts = ring_gather(cache[:HALF], cache[HALF:], lambda v, d: move_seq(v, 0, d))

    og_rel = masked_grads(base, context_grad)
    og_parts = spread([og_rel[n] for n in range(4)])

    half = hidden.shape[1] // 2
    before, after = move_tp(hidden, 1, 0), move_tp(hidden, -1, 0)
    group = [hidden, before, after, move_tp(before[:, :half], 1, 0), move_tp(after[:, half:], -1, 0)]
    pieces = group + [move_tp(v, 0, 1) for v in group]
    q_rel, k, v = project(base, pieces, wq, wk, wv, og_rel)
    q_parts = spread([q_rel[n] for n in range(4)])

    dq_dense, ctx_dense, q_all, og_all, a, ds = work(meta, q_parts, og_parts, kv_parts)
    dq_parts = send_back(dq_dense)

    grad = functools.partial(cache_grad, a=a, ds=ds, q_all=q_all, og_all=og_all)
    far_a, far_b = grad(3)
    got_a, got_b = move_seq(far_a, 0, 1), move_seq(far_b, 0, -1)
    prev_a, prev_b = grad(1)
    next_a, next_b = grad(2)
    own_a, own_b = grad(0)
    add = lambda *terms: sum(t.astype(F32) for t in terms).astype(BF)
    from_prev_b = move_seq(next_b, 0, 1)
    from_next_a = move_seq(prev_a, 0, -1)
    from_prev_a = move_seq(add(next_a, got_a), 0, 1)
    from_next_b = move_seq(add(prev_b, got_b), 0, -1)
    prefix_grad = jnp.concatenate([add(own_a, from_prev_a, from_next_a), add(own_b, from_prev_b, from_next_b)])
    prefix_grad = prefix_grad.reshape(CHUNK, 1, 2, HD)

    parts = hidden_grad_parts(base, dq_parts, q_rel, og_rel, k, v, wq, wk, wv)
    pair = add(parts[0], move_tp(parts[1], 0, 1))
    hidden_grad = add(pair[0], *[move_tp(pair[n], n, 0) for n in (1, 2, 3)])

    ctx_parts = send_back(ctx_dense)
    context = finish_context(base, ctx_parts, q_rel, k, v, dq_parts)
    return context, hidden_grad, prefix_grad


def solution(mesh):
    return jax.shard_map(
        on_device,
        mesh=mesh,
        in_specs=(
            P(("seq", "tp"), None),
            P(None, "tp"),
            P(None, "tp"),
            P(None, "tp"),
            P("seq", "tp", None, None),
            P("seq"),
            P("seq"),
            P("seq", "tp"),
        ),
        out_specs=(P("seq", "tp"), P(("seq", "tp"), None), P("seq", "tp", None, None)),
        check_vma=False,
    )
```

```python
import functools
import math

import jax
import jax.numpy as jnp
from jax import lax
from jax.experimental import pallas as pl
from jax.experimental.pallas import tpu as pltpu
from jax.sharding import PartitionSpec as P

HD = 128
RESP_LEN = 32
ROWS = 128
SLICE = 256
STAT_ROWS = 16
CHUNK = 2048
HALF = 1024
PARTS = 5
KEYS = 8192
WROWS = 1024
BLOCK = 1024
SCALE = HD ** -0.5
EXP2_SCALE = SCALE * math.log2(math.e)
NEG = -1.0e30
BF = jnp.bfloat16
F32 = jnp.float32
NT = (((1,), (1,)), ((), ()))
NN = (((1,), (0,)), ((), ()))
TN = (((0,), (0,)), ((), ()))
ANY = pl.BlockSpec(memory_space=pl.ANY)
VM = pl.BlockSpec(memory_space=pltpu.VMEM)
SM = pl.BlockSpec(memory_space=pltpu.SMEM)
XG = [[a * 4 + b for a in range(4)] for b in range(4)]
YG = [[a * 4 + b for b in range(4)] for a in range(4)]


def dot(a, b, dims):
    return lax.dot_general(a, b, dims, preferred_element_type=F32)


def move_tp(x, dz, dc):
    pairs = [(z * 2 + c, ((z + dz) % 4) * 2 + (c + dc) % 2) for z in range(4) for c in range(2)]
    return lax.ppermute(x, "tp", pairs)


def move_seq(x, dx, dy):
    pairs = [(a * 4 + b, ((a + dx) % 4) * 4 + (b + dy) % 4) for a in range(4) for b in range(4)]
    return lax.ppermute(x, "seq", pairs)


def split3(v):
    hi = v.astype(BF).astype(F32)
    mid = (v - hi).astype(BF).astype(F32)
    return hi, mid, v - hi - mid


def stat_rows(first, second):
    rows = list(split3(first)) + list(split3(second))
    return jnp.concatenate(rows + [jnp.zeros((STAT_ROWS - 6, SLICE), F32)], axis=0).astype(BF)


def read_stats(rows):
    r = rows.astype(F32)
    return r[0:1] + r[1:2] + r[2:3], r[3:4] + r[4:5] + r[5:6]


def causal_mask(lens):
    key = lax.broadcasted_iota(jnp.int32, (ROWS, ROWS), 0)
    row = lax.broadcasted_iota(jnp.int32, (ROWS, ROWS), 1)
    member = lax.shift_right_logical(key, 5)
    length = jnp.where(member == 0, lens[0], jnp.where(member == 1, lens[1], jnp.where(member == 2, lens[2], lens[3])))
    live = (key & (RESP_LEN - 1)) < length
    return (member == lax.shift_right_logical(row, 5)) & (key <= row) & live


def wide_mask(meta):
    return jnp.concatenate([causal_mask([meta[4], meta[5], meta[6], meta[7]])] * 8, axis=1)


def stack(slices, into):
    for at in range(4):
        for j in range(2):
            n = (at * 2 + j) * HD
            into[n:n + HD] = slices[at, :ROWS, j * HD:(j + 1) * HD]


def stack_turned(y, slices, into):
    for n in range(4):
        for j in range(2):
            start = pl.multiple_of((((y + n) & 3) * 2 + j) * HD, HD)
            into[pl.ds(start, HD)] = slices[n][:ROWS, j * HD:(j + 1) * HD]


def live_rows(meta, shape):
    row = lax.broadcasted_iota(jnp.int32, shape, 0)
    member = lax.shift_right_logical(row, 5)
    length = jnp.where(member == 0, meta[4], jnp.where(member == 1, meta[5], jnp.where(member == 2, meta[6], meta[7])))
    return (row & (RESP_LEN - 1)) < length


def group_kernel(a, b, c, d, out):
    for n, piece in enumerate((a, b, c, d)):
        out[n * 16:(n + 1) * 16] = piece[...]


def group_rows(pieces):
    return pl.pallas_call(
        group_kernel,
        in_specs=[VM] * 4,
        out_specs=VM,
        out_shape=jax.ShapeDtypeStruct((64, pieces[0].shape[1]), BF),
        compiler_params=pltpu.CompilerParams(vmem_limit_bytes=6 << 20),
        name="group_rows",
    )(*pieces)


def near_kernel(*refs):
    ins, outs, sem = refs[:3], refs[-4:-1], refs[-1]
    copies = [pltpu.make_async_copy(src, dst, sem.at[n]) for n, (src, dst) in enumerate(zip(ins, outs))]
    for copy in copies:
        copy.start()
    for copy in copies:
        copy.wait()


def bring_near(weights, after=()):
    d = weights[0].shape[0]
    return pl.pallas_call(
        near_kernel,
        in_specs=[ANY] * (3 + len(after)),
        out_specs=[VM] * 3,
        out_shape=[pltpu.VMEM(w.shape, BF) for w in weights],
        scratch_shapes=[pltpu.SemaphoreType.DMA((3,))],
        compiler_params=pltpu.CompilerParams(vmem_limit_bytes=4 << 20),
        cost_estimate=pl.CostEstimate(flops=0, bytes_accessed=d * 2560, transcendentals=0),
        name="bring_near",
    )(*weights, *after)


def project_kernel(meta, *refs):
    pieces, (wq_s, wk_s, wv_s), cg = refs[:2], refs[2:5], refs[5]
    out, k_out, v_out, og = refs[6], refs[7], refs[8], refs[9:13]
    seg, q_all, og_all, sem = refs[13:]
    z, c = meta[2], meta[3]
    copies = []
    for rc in range(2):
        for dz in range(4):
            start = pl.multiple_of((((z - dz) & 3) * 2 + (c ^ rc)) * 16, 16)
            source = pieces[rc].at[pl.ds(dz * 16, 16)]
            copies.append(pltpu.make_async_copy(source, seg.at[pl.ds(start, 16)], sem.at[rc * 4 + dz]))
    for copy in copies:
        copy.start()
    live = live_rows(meta, (ROWS, SLICE))
    prompt = jnp.full((STAT_ROWS, SLICE), meta[8], jnp.int32).astype(F32).astype(BF)
    for n in range(4):
        start = pl.multiple_of(((meta[1] + n) & 3) * SLICE, SLICE)
        grads = cg[:, pl.ds(start, SLICE)]
        og[n][:ROWS] = jnp.where(live, grads, jnp.zeros_like(grads))
        og[n][ROWS:] = prompt
    stack_turned(meta[1], og, og_all)
    for copy in copies:
        copy.wait()
    k_out[...] = dot(seg[...], wk_s[...], NN).astype(BF)
    v_out[...] = dot(seg[...], wv_s[...], NN).astype(BF)
    q = dot(seg[...], wq_s[...], NN).astype(BF)
    for h in range(8):
        q_all[h * HD:(h + 1) * HD] = q[:, h * HD:(h + 1) * HD]
    mask = wide_mask(meta)
    s = jnp.where(mask, dot(k_out[...], q_all[...], NT) * SCALE, NEG)
    top = jnp.max(s, axis=0, keepdims=True)
    p = jnp.where(mask, jnp.exp(s - top), 0.0)
    total = jnp.sum(p, axis=0, keepdims=True)
    dp = dot(v_out[...], og_all[...], NT)
    lse = top + jnp.log(total)
    corr = jnp.sum(p.astype(BF).astype(F32) * dp, axis=0, keepdims=True) / total
    for at in range(4):
        cols = slice(at * SLICE, (at + 1) * SLICE)
        stats = stat_rows(lse[:, cols], corr[:, cols])
        out[at, :ROWS] = q[:, cols]
        out[at, ROWS:] = stats


def project(meta, pieces, wq, wk, wv, context_grad):
    d = wq.shape[0]
    return pl.pallas_call(
        project_kernel,
        in_specs=[SM] + [ANY] * 2 + [VM] * 4,
        out_specs=[VM] * 7,
        scratch_shapes=[
            pltpu.VMEM((ROWS, d), BF),
            pltpu.VMEM((WROWS, HD), BF),
            pltpu.VMEM((WROWS, HD), BF),
            pltpu.SemaphoreType.DMA((8,)),
        ],
        out_shape=[
            jax.ShapeDtypeStruct((4, ROWS + STAT_ROWS, SLICE), BF),
            jax.ShapeDtypeStruct((ROWS, HD), BF),
            jax.ShapeDtypeStruct((ROWS, HD), BF),
        ] + [jax.ShapeDtypeStruct((ROWS + STAT_ROWS, SLICE), BF)] * 4,
        compiler_params=pltpu.CompilerParams(vmem_limit_bytes=16 << 20),
        cost_estimate=pl.CostEstimate(flops=2 * ROWS * d * 1280, bytes_accessed=d * 1280 * 2, transcendentals=0),
        name="project",
    )(meta, *pieces, wq, wk, wv, context_grad)


def pack_kernel(q, g0, g1, g2, g3, out, h0, h1, h2, h3, sem):
    copies = [pltpu.make_async_copy(q, out.at[n], sem.at[n]) for n in range(4)]
    for copy in copies:
        copy.start()
    for src, dst in ((g0, h0), (g1, h1), (g2, h2), (g3, h3)):
        dst[...] = src[...]
    for copy in copies:
        copy.wait()


def pack(q, og):
    return pl.pallas_call(
        pack_kernel,
        in_specs=[VM] * 5,
        out_specs=[ANY] + [VM] * 4,
        out_shape=[jax.ShapeDtypeStruct((4,) + q.shape, BF)] + [jax.ShapeDtypeStruct(g.shape, BF) for g in og],
        scratch_shapes=[pltpu.SemaphoreType.DMA((4,))],
        compiler_params=pltpu.CompilerParams(vmem_limit_bytes=8 << 20),
        name="pack",
    )(q, *og)


def forward_kernel(sel, q_in, *refs):
    og_in, kv_in, refs = refs[:4], refs[4], refs[5:]
    ctx_out, q_all, og_all, scale_out, stat_out, p_hbm = refs[:6]
    qslot, ogslot, kv, p_all, s_even, s_odd, acc, mblk, m_ref, l_ref, sem_in, sem_kv, sem_out = refs[6:]
    blocks = KEYS // BLOCK

    kv_copies = kv_copies_of(kv_in, kv, sem_kv)
    copies, waits = [], []
    for r in range(4):
        copies.append(pltpu.make_async_copy(q_in.at[sel[r]], qslot.at[r], sem_in.at[r]))
        for n in range(4):
            @pl.when(sel[4 + r] == n)
            def _():
                pltpu.make_async_copy(og_in[n].at[sel[8 + r]], ogslot.at[r], sem_in.at[4 + r]).start()
        waits.append(pltpu.make_async_copy(og_in[0].at[0], ogslot.at[r], sem_in.at[4 + r]))
    for copy in copies:
        copy.start()
    for copy in kv_copies:
        copy.start()
    ctx_out[...] = jnp.zeros_like(ctx_out)
    m_ref[...] = jnp.full_like(m_ref, NEG)
    l_ref[...] = jnp.zeros_like(l_ref)
    acc[...] = jnp.zeros_like(acc)
    for copy in copies + waits:
        copy.wait()
    stack(qslot, q_all)
    stack(ogslot, og_all)

    def scores(b, into):
        keys = pl.ds(pl.multiple_of(b * BLOCK, BLOCK), BLOCK)
        into[...] = dot(kv[keys, :HD], q_all[...], NT)

    def soften(b, scored):
        keys = pl.ds(pl.multiple_of(b * BLOCK, BLOCK), BLOCK)
        s = scored[...]
        old = m_ref[...]
        new = jnp.maximum(old, jnp.max(s, axis=0, keepdims=True))
        p = jnp.exp2((s - new) * EXP2_SCALE)
        factor = jnp.exp2((old - new) * EXP2_SCALE)
        l_ref[...] = l_ref[...] * factor + jnp.sum(p, axis=0, keepdims=True)
        pb = p.astype(BF)
        p_all[keys, :] = pb
        pltpu.make_async_copy(p_all.at[keys], p_hbm.at[keys], sem_out.at[b]).start()
        acc[...] = acc[...] * factor + dot(kv[keys, HD:].T, pb, NN)
        m_ref[...] = new
        mblk[pl.ds(b, 1), :] = new

    kv_arrived(0, kv_in, kv, sem_kv)
    scores(0, s_even)

    def forward(b, _):
        kv_arrived(2 * b + 1, kv_in, kv, sem_kv)
        scores(2 * b + 1, s_odd)
        soften(2 * b, s_even)

        @pl.when(b < blocks // 2 - 1)
        def _():
            kv_arrived(2 * b + 2, kv_in, kv, sem_kv)
        scores(lax.rem(2 * b + 2, blocks), s_even)
        soften(2 * b + 1, s_odd)
        return 0

    lax.fori_loop(0, blocks // 2, forward, 0)

    for r in range(4):
        rs = slice(r * SLICE, (r + 1) * SLICE)
        lse0, corr0 = read_stats(qslot[r, ROWS:])
        lse = m_ref[:, rs] * SCALE + jnp.log(l_ref[:, rs])
        top = jnp.maximum(lse, lse0)
        log_norm = top + jnp.log(jnp.exp(lse - top) + jnp.exp(lse0 - top))
        inv = jnp.exp(lse - log_norm) / l_ref[:, rs]
        ctx = acc[:, rs] * inv
        ogt = og_all[rs].astype(F32).T
        corr = jnp.sum(ogt * ctx, axis=0, keepdims=True) + corr0 * jnp.exp(lse0 - log_norm)
        ctx_rows = ctx.T
        for j in range(2):
            ctx_out[sel[r], :, j * HD:(j + 1) * HD] = ctx_rows[j * HD:(j + 1) * HD].astype(BF)
        stat_out[0:1, rs] = log_norm
        stat_out[1:2, rs] = corr
        scale_out[:, rs] = jnp.exp2((mblk[:, rs] - m_ref[:, rs]) * EXP2_SCALE) * inv
    for b in range(blocks):
        keys = pl.ds(b * BLOCK, BLOCK)
        pltpu.make_async_copy(p_all.at[keys], p_hbm.at[keys], sem_out.at[b]).wait()


def kv_copies_of(kv_in, kv, sem):
    blocks = [pl.ds(n * BLOCK, BLOCK) for n in range(KEYS // BLOCK)]
    return [pltpu.make_async_copy(kv_in.at[rows], kv.at[rows], sem.at[n]) for n, rows in enumerate(blocks)]


def kv_arrived(b, kv_in, kv, sem):
    keys = pl.ds(pl.multiple_of(b * BLOCK, BLOCK), BLOCK)
    pltpu.make_async_copy(kv_in.at[keys], kv.at[keys], sem.at[b]).wait()


def backward_kernel(sel, q_all, og_all, factors, stats, p_hbm, *refs):
    kv_in, refs = refs[0], refs[1:]
    dq_out, dkv_out, kv, dkv, p_all, dqt, sem_kv, sem_p, sem_out = refs
    blocks = KEYS // BLOCK
    kv_copies = kv_copies_of(kv_in, kv, sem_kv)
    for b in range(blocks):
        keys = pl.ds(b * BLOCK, BLOCK)
        kv_copies[b].start()
        pltpu.make_async_copy(p_hbm.at[keys], p_all.at[keys], sem_p.at[b]).start()
    dq_out[...] = jnp.zeros_like(dq_out)
    dqt[...] = jnp.zeros_like(dqt)
    corr = stats[1:2]

    def backward(b, _):
        keys = pl.ds(pl.multiple_of(b * BLOCK, BLOCK), BLOCK)
        kv_arrived(b, kv_in, kv, sem_kv)
        dp = dot(kv[keys, HD:], og_all[...], NT)
        pltpu.make_async_copy(p_hbm.at[keys], p_all.at[keys], sem_p.at[b]).wait()
        a = p_all[keys, :].astype(F32) * factors[pl.ds(b, 1), :]
        ds = (a * (dp - corr)).astype(BF)
        dkv[keys, HD:] = dot(a.astype(BF), og_all[...], NN).astype(BF)
        dkv[keys, :HD] = (dot(ds, q_all[...], NN) * SCALE).astype(BF)
        pltpu.make_async_copy(dkv.at[keys], dkv_out.at[keys], sem_out.at[b]).start()
        dqt[...] += dot(kv[keys, :HD].T, ds, NN)
        return 0

    lax.fori_loop(0, blocks, backward, 0)
    for r in range(4):
        rs = slice(r * SLICE, (r + 1) * SLICE)
        rows = (dqt[:, rs] * SCALE).T
        for j in range(2):
            dq_out[sel[r], :ROWS, j * HD:(j + 1) * HD] = rows[j * HD:(j + 1) * HD].astype(BF)
        dq_out[sel[r], ROWS:] = stat_rows(stats[0:1, rs], stats[1:2, rs])
    for b in range(blocks):
        keys = pl.ds(b * BLOCK, BLOCK)
        pltpu.make_async_copy(dkv.at[keys], dkv_out.at[keys], sem_out.at[b]).wait()


def forward(sel, q_parts, og_parts, kv):
    blocks = KEYS // BLOCK
    return pl.pallas_call(
        forward_kernel,
        in_specs=[SM] + [ANY] * 6,
        out_specs=[VM] * 5 + [ANY],
        out_shape=[
            jax.ShapeDtypeStruct((16, ROWS, SLICE), BF),
            jax.ShapeDtypeStruct((WROWS, HD), BF),
            jax.ShapeDtypeStruct((WROWS, HD), BF),
            jax.ShapeDtypeStruct((blocks, WROWS), F32),
            jax.ShapeDtypeStruct((2, WROWS), F32),
            jax.ShapeDtypeStruct((KEYS, WROWS), BF),
        ],
        scratch_shapes=[
            pltpu.VMEM((4, ROWS + STAT_ROWS, SLICE), BF),
            pltpu.VMEM((4, ROWS + STAT_ROWS, SLICE), BF),
            pltpu.VMEM((KEYS, SLICE), BF),
            pltpu.VMEM((KEYS, WROWS), BF),
            pltpu.VMEM((BLOCK, WROWS), F32),
            pltpu.VMEM((BLOCK, WROWS), F32),
            pltpu.VMEM((HD, WROWS), F32),
            pltpu.VMEM((blocks, WROWS), F32),
            pltpu.VMEM((1, WROWS), F32),
            pltpu.VMEM((1, WROWS), F32),
            pltpu.SemaphoreType.DMA((8,)),
            pltpu.SemaphoreType.DMA((8,)),
            pltpu.SemaphoreType.DMA((blocks,)),
        ],
        compiler_params=pltpu.CompilerParams(vmem_limit_bytes=58 << 20),
        cost_estimate=pl.CostEstimate(flops=4 * WROWS * KEYS * HD, bytes_accessed=22 << 20, transcendentals=WROWS * KEYS),
        name="attention_forward",
    )(sel, q_parts, *og_parts, kv)


def backward(sel, q_all, og_all, factors, stats, p, kv):
    blocks = KEYS // BLOCK
    return pl.pallas_call(
        backward_kernel,
        in_specs=[SM] + [VM] * 4 + [ANY] * 2,
        out_specs=[VM, ANY],
        out_shape=[
            jax.ShapeDtypeStruct((16, ROWS + STAT_ROWS, SLICE), BF),
            jax.ShapeDtypeStruct((KEYS, SLICE), BF),
        ],
        scratch_shapes=[
            pltpu.VMEM((KEYS, SLICE), BF),
            pltpu.VMEM((KEYS, SLICE), BF),
            pltpu.VMEM((KEYS, WROWS), BF),
            pltpu.VMEM((HD, WROWS), F32),
            pltpu.SemaphoreType.DMA((8,)),
            pltpu.SemaphoreType.DMA((blocks,)),
            pltpu.SemaphoreType.DMA((blocks,)),
        ],
        compiler_params=pltpu.CompilerParams(vmem_limit_bytes=58 << 20),
        cost_estimate=pl.CostEstimate(flops=8 * WROWS * KEYS * HD, bytes_accessed=24 << 20, transcendentals=0),
        name="attention_backward",
    )(sel, q_all, og_all, factors, stats, p, kv)


def hidden_kernel(meta, dq_in, qs, og0, og1, og2, og3, k, v, wq, wk, wv, out, q_all, og_all, dq_got, dq_s, dk_s, dv_s, part, sem):
    fetch = pltpu.make_async_copy(dq_in.at[meta[8]], dq_got, sem.at[0])
    fetch.start()
    size = part.shape[1]
    stack(qs, q_all)
    stack_turned(meta[1], (og0, og1, og2, og3), og_all)
    mask = wide_mask(meta)
    s = dot(k[...], q_all[...], NT) * SCALE
    dp = dot(v[...], og_all[...], NT)
    fetch.wait()
    stats = [read_stats(dq_got[at, ROWS:]) for at in range(4)]
    log_norm = jnp.concatenate([t[0] for t in stats], axis=1)
    corr = jnp.concatenate([t[1] for t in stats], axis=1)
    a = jnp.where(mask, jnp.exp(jnp.where(mask, s - log_norm, 0.0)), 0.0)
    ds = (a * (dp - corr)).astype(BF)
    dk_s[...] = (dot(ds, q_all[...], NN) * SCALE).astype(BF)
    dv_s[...] = dot(a.astype(BF), og_all[...], NN).astype(BF)
    for h in range(8):
        cols = slice(h % 2 * HD, (h % 2 + 1) * HD)
        own = dot(ds[:, h * HD:(h + 1) * HD], k[...], TN) * SCALE
        dq_s[:, h * HD:(h + 1) * HD] = (dq_got[h // 2, :ROWS, cols].astype(F32) + own).astype(BF)

    z, c = meta[2], meta[3]
    for n in range(PARTS):
        at = slice(n * size, (n + 1) * size)
        part[...] = dot(dq_s[...], wq[at], NT) + dot(dk_s[...], wk[at], NT) + dot(dv_s[...], wv[at], NT)
        for rc in range(2):
            for dz in range(4):
                start = pl.multiple_of((((z + dz) & 3) * 2 + (c ^ rc)) * 16, 16)
                out[rc, dz, :, at] = part[pl.ds(start, 16), :].astype(BF)


def hidden_grad_parts(meta, dq, q, og, k, v, wq, wk, wv):
    d = wq.shape[0]
    return pl.pallas_call(
        hidden_kernel,
        in_specs=[SM, ANY] + [VM] * 10,
        out_specs=VM,
        scratch_shapes=[
            pltpu.VMEM((WROWS, HD), BF),
            pltpu.VMEM((WROWS, HD), BF),
            pltpu.VMEM((4, ROWS + STAT_ROWS, SLICE), BF),
            pltpu.VMEM((ROWS, 1024), BF),
            pltpu.VMEM((ROWS, HD), BF),
            pltpu.VMEM((ROWS, HD), BF),
            pltpu.VMEM((ROWS, d // PARTS), F32),
            pltpu.SemaphoreType.DMA((1,)),
        ],
        out_shape=jax.ShapeDtypeStruct((2, 4, 16, d), BF),
        compiler_params=pltpu.CompilerParams(vmem_limit_bytes=16 << 20),
        cost_estimate=pl.CostEstimate(flops=2 * ROWS * d * 1280, bytes_accessed=d * 1280 * 2, transcendentals=0),
        name="hidden_grad",
    )(meta, dq, q, *og, k, v, wq, wk, wv)


def context_kernel(meta, ctx, q, k, v, dq, after, out, q_all):
    stack(q, q_all)
    log_norm = jnp.concatenate([read_stats(dq[0, at, ROWS:])[0] for at in range(4)], axis=1)
    mask = wide_mask(meta)
    live = live_rows(meta, (ROWS, HD))
    s = dot(k[...], q_all[...], NT) * SCALE
    a = jnp.where(mask, jnp.exp(jnp.where(mask, s - log_norm, 0.0)), 0.0).astype(BF)
    for h in range(8):
        cols = slice(h % 2 * HD, (h % 2 + 1) * HD)
        own = dot(a[:, h * HD:(h + 1) * HD], v[...], TN)
        out[:, h * HD:(h + 1) * HD] = jnp.where(live, ctx[h // 2, :, cols].astype(F32) + own, 0.0).astype(BF)


def finish_context(meta, ctx, q, k, v, dq, after):
    rows = ROWS + STAT_ROWS
    return pl.pallas_call(
        context_kernel,
        grid_spec=pltpu.PrefetchScalarGridSpec(
            num_scalar_prefetch=1,
            grid=(1,),
            in_specs=[
                pl.BlockSpec((4, ROWS, SLICE), lambda i, m: (0, 0, 0)),
                pl.BlockSpec((4, rows, SLICE), lambda i, m: (0, 0, 0)),
                pl.BlockSpec((ROWS, HD), lambda i, m: (0, 0)),
                pl.BlockSpec((ROWS, HD), lambda i, m: (0, 0)),
                pl.BlockSpec((1, 4, rows, SLICE), lambda i, m: (m[8], 0, 0, 0)),
                ANY,
            ],
            out_specs=pl.BlockSpec((ROWS, 1024), lambda i, m: (0, 0)),
            scratch_shapes=[pltpu.VMEM((WROWS, HD), BF)],
        ),
        out_shape=jax.ShapeDtypeStruct((ROWS, 1024), BF),
        compiler_params=pltpu.CompilerParams(vmem_limit_bytes=16 << 20),
        name="context",
    )(meta, ctx, q, k, v, dq, after)


def exchange(parts):
    return lax.all_to_all(parts.reshape(16, -1, SLICE), "seq", 0, 0, tiled=True)


def add(*terms):
    return sum(t.astype(F32) for t in terms).astype(BF)


def on_device(hidden, wq, wk, wv, prefix_cache, owner_prompt, response_length, context_grad):
    seq, tp = lax.axis_index("seq"), lax.axis_index("tp")
    x, y, z, c = seq // 4, seq % 4, tp // 2, tp % 2
    place = jnp.stack([x, y, z, c]).astype(jnp.int32)
    meta = jnp.concatenate([place, response_length, owner_prompt])

    kv = lax.all_gather(prefix_cache.reshape(CHUNK, SLICE), "seq", axis=0, tiled=True, axis_index_groups=YG)

    passed = [move_tp(hidden, n, 0) for n in (1, 2, 3)]
    group = group_rows([hidden] + passed)
    near = bring_near((wq, wk, wv), (group,))
    q, k, v, *og = project(meta, [group, move_tp(group, 0, 1)], *near, context_grad)
    packed, *og = pack(q, og)
    q_parts = exchange(packed)
    og_row = jnp.stack([og[0]] + [move_seq(og[n], 0, n) for n in (1, 2, 3)])
    og_parts = [og_row] + [move_seq(og_row, n, 0) for n in (1, 2, 3)]

    prompts = jnp.concatenate([part[:, ROWS, 0] for part in og_parts]).astype(jnp.int32)
    owners = jnp.arange(16, dtype=jnp.int32)
    match = prompts == x
    owner = (x - owners // 4) % 4 * 4 + (y - owners) % 4
    rank = jnp.sum(match[None, :] & (owners[None, :] < owners[:, None]), axis=1)
    chosen = match[None, :] & (rank[None, :] == jnp.arange(4)[:, None])
    sel = jnp.sum(jnp.where(chosen, owner[None, :], 0), axis=1)
    spot = jnp.sum(jnp.where(chosen, owners[None, :], 0), axis=1)
    sel = jnp.concatenate([sel, spot // 4, spot % 4]).astype(jnp.int32)

    ctx_dense, q_all, og_all, factors, stats, weights = forward(sel, q_parts, og_parts, kv)
    ctx_row = lax.psum_scatter(ctx_dense.reshape(-1, SLICE), "seq", scatter_dimension=0, tiled=True, axis_index_groups=XG)
    dq_dense, dkv = backward(sel, q_all, og_all, factors, stats, weights, kv)
    dq = exchange(dq_dense).reshape(4, 4, ROWS + STAT_ROWS, SLICE)
    prefix_grad = lax.psum_scatter(dkv, "seq", scatter_dimension=0, tiled=True, axis_index_groups=YG)
    prefix_grad = prefix_grad.reshape(CHUNK, 1, 2, HD)

    parts = hidden_grad_parts(meta, dq, q, og, k, v, wq, wk, wv)
    pair = add(parts[0], move_tp(parts[1], 0, 1))
    hidden_grad = add(pair[0], *[move_tp(pair[n], n, 0) for n in (1, 2, 3)])

    ctx_parts = lax.all_to_all(ctx_row.reshape(4, ROWS, SLICE), "seq", 0, 0, tiled=True, axis_index_groups=YG)
    context = finish_context(meta, ctx_parts, q, k, v, dq, parts)
    return context, hidden_grad, prefix_grad


def solution(mesh):
    return jax.shard_map(
        on_device,
        mesh=mesh,
        in_specs=(
            P(("seq", "tp"), None),
            P(None, "tp"),
            P(None, "tp"),
            P(None, "tp"),
            P("seq", "tp", None, None),
            P("seq"),
            P("seq"),
            P("seq", "tp"),
        ),
        out_specs=(P("seq", "tp"), P(("seq", "tp"), None), P("seq", "tp", None, None)),
        check_vma=False,
    )
```

```python
import functools
import math

import jax
import jax.numpy as jnp
from jax import lax
from jax.experimental import pallas as pl
from jax.experimental.pallas import tpu as pltpu
from jax.sharding import PartitionSpec as P

HD = 128
RESP_LEN = 32
ROWS = 128
SLICE = 256
STAT_ROWS = 16
PART_ROWS = ROWS + STAT_ROWS
CHUNK = 2048
HALF = 1024
PARTS = 5
KEYS = 8192
WROWS = 1024
BLOCK = 1024
WIDE = 2048
SCALE = HD ** -0.5
EXP2_SCALE = SCALE * math.log2(math.e)
NEG = -1.0e30
BF = jnp.bfloat16
F32 = jnp.float32
NT = (((1,), (1,)), ((), ()))
NN = (((1,), (0,)), ((), ()))
TN = (((0,), (0,)), ((), ()))
ANY = pl.BlockSpec(memory_space=pl.ANY)
VM = pl.BlockSpec(memory_space=pltpu.VMEM)
SM = pl.BlockSpec(memory_space=pltpu.SMEM)
XG = [[a * 4 + b for a in range(4)] for b in range(4)]
YG = [[a * 4 + b for b in range(4)] for a in range(4)]


def dot(a, b, dims):
    return lax.dot_general(a, b, dims, preferred_element_type=F32)


def move_tp(x, dz, dc):
    pairs = [(z * 2 + c, ((z + dz) % 4) * 2 + (c + dc) % 2) for z in range(4) for c in range(2)]
    return lax.ppermute(x, "tp", pairs)


def move_seq(x, dx, dy):
    pairs = [(a * 4 + b, ((a + dx) % 4) * 4 + (b + dy) % 4) for a in range(4) for b in range(4)]
    return lax.ppermute(x, "seq", pairs)


def ring_gather(a, b, move):
    pa, nb = move(a, 1), move(b, -1)
    pb, na = move(b, 1), move(a, -1)
    return [a, b, pa, pb, na, nb, move(pa, 1), move(nb, -1)]


def split3(v):
    hi = v.astype(BF).astype(F32)
    mid = (v - hi).astype(BF).astype(F32)
    return hi, mid, v - hi - mid


def stat_rows(first, second):
    rows = list(split3(first)) + list(split3(second))
    return jnp.concatenate(rows + [jnp.zeros((STAT_ROWS - 6, SLICE), F32)], axis=0).astype(BF)


def read_stats(rows):
    r = rows.astype(F32)
    return r[0:1] + r[1:2] + r[2:3], r[3:4] + r[4:5] + r[5:6]


def causal_mask(lens):
    key = lax.broadcasted_iota(jnp.int32, (ROWS, ROWS), 0)
    row = lax.broadcasted_iota(jnp.int32, (ROWS, ROWS), 1)
    member = lax.shift_right_logical(key, 5)
    length = jnp.where(member == 0, lens[0], jnp.where(member == 1, lens[1], jnp.where(member == 2, lens[2], lens[3])))
    live = (key & (RESP_LEN - 1)) < length
    return (member == lax.shift_right_logical(row, 5)) & (key <= row) & live


def wide_mask(meta):
    return jnp.concatenate([causal_mask([meta[4], meta[5], meta[6], meta[7]])] * 8, axis=1)


def stack_turned(y, slices, into, first):
    for n in range(4):
        for j in range(2):
            start = pl.multiple_of((((y + n) & 3) * 2 + j) * HD, HD)
            into[pl.ds(start, HD)] = slices[n][first:first + ROWS, j * HD:(j + 1) * HD]


def live_rows(meta, shape):
    row = lax.broadcasted_iota(jnp.int32, shape, 0)
    member = lax.shift_right_logical(row, 5)
    length = jnp.where(member == 0, meta[4], jnp.where(member == 1, meta[5], jnp.where(member == 2, meta[6], meta[7])))
    return (row & (RESP_LEN - 1)) < length


def group_kernel(a, b, c, d, out):
    for n, piece in enumerate((a, b, c, d)):
        out[n * 16:(n + 1) * 16] = piece[...]


def group_rows(pieces):
    return pl.pallas_call(
        group_kernel,
        in_specs=[VM] * 4,
        out_specs=VM,
        out_shape=jax.ShapeDtypeStruct((64, pieces[0].shape[1]), BF),
        compiler_params=pltpu.CompilerParams(vmem_limit_bytes=6 << 20),
        name="group_rows",
    )(*pieces)


def near_kernel(*refs):
    ins, outs, sem = refs[:3], refs[-4:-1], refs[-1]
    copies = [pltpu.make_async_copy(src, dst, sem.at[n]) for n, (src, dst) in enumerate(zip(ins, outs))]
    for copy in copies:
        copy.start()
    for copy in copies:
        copy.wait()


def bring_near(weights, after=()):
    d = weights[0].shape[0]
    return pl.pallas_call(
        near_kernel,
        in_specs=[ANY] * (3 + len(after)),
        out_specs=[VM] * 3,
        out_shape=[pltpu.VMEM(w.shape, BF) for w in weights],
        scratch_shapes=[pltpu.SemaphoreType.DMA((3,))],
        compiler_params=pltpu.CompilerParams(vmem_limit_bytes=4 << 20),
        cost_estimate=pl.CostEstimate(flops=0, bytes_accessed=d * 2560, transcendentals=0),
        name="bring_near",
    )(*weights, *after)


def project_kernel(meta, *refs):
    pieces, (wq_s, wk_s, wv_s), cg = refs[:2], refs[2:5], refs[5]
    k_out, v_out, pay = refs[6], refs[7], refs[8:12]
    seg, q_all, og_all, q_s, stat_s, sem = refs[12:]
    z, c = meta[2], meta[3]
    copies = []
    for rc in range(2):
        for dz in range(4):
            start = pl.multiple_of((((z - dz) & 3) * 2 + (c ^ rc)) * 16, 16)
            source = pieces[rc].at[pl.ds(dz * 16, 16)]
            copies.append(pltpu.make_async_copy(source, seg.at[pl.ds(start, 16)], sem.at[rc * 4 + dz]))
    for copy in copies:
        copy.start()
    live = live_rows(meta, (ROWS, SLICE))
    prompt = jnp.full((STAT_ROWS, SLICE), meta[8], jnp.int32).astype(F32).astype(BF)
    for n in range(4):
        start = pl.multiple_of(((meta[1] + n) & 3) * SLICE, SLICE)
        grads = cg[:, pl.ds(start, SLICE)]
        pay[n][PART_ROWS:PART_ROWS + ROWS] = jnp.where(live, grads, jnp.zeros_like(grads))
        pay[n][PART_ROWS + ROWS:] = prompt
    stack_turned(meta[1], pay, og_all, PART_ROWS)
    for copy in copies:
        copy.wait()
    k_out[...] = dot(seg[...], wk_s[...], NN).astype(BF)
    v_out[...] = dot(seg[...], wv_s[...], NN).astype(BF)
    q = dot(seg[...], wq_s[...], NN).astype(BF)
    q_s[...] = q
    for h in range(8):
        q_all[h * HD:(h + 1) * HD] = q[:, h * HD:(h + 1) * HD]
    mask = wide_mask(meta)
    s = jnp.where(mask, dot(k_out[...], q_all[...], NT) * SCALE, NEG)
    top = jnp.max(s, axis=0, keepdims=True)
    p = jnp.where(mask, jnp.exp(s - top), 0.0)
    total = jnp.sum(p, axis=0, keepdims=True)
    dp = dot(v_out[...], og_all[...], NT)
    lse = top + jnp.log(total)
    corr = jnp.sum(p.astype(BF).astype(F32) * dp, axis=0, keepdims=True) / total
    stat_s[0:1] = lse
    stat_s[1:2] = corr
    for n in range(4):
        cols = pl.ds(pl.multiple_of(((meta[1] + n) & 3) * SLICE, SLICE), SLICE)
        pay[n][:ROWS] = q_s[:, cols]
        pay[n][ROWS:PART_ROWS] = stat_rows(stat_s[0:1, cols], stat_s[1:2, cols])


def project(meta, pieces, wq, wk, wv, context_grad):
    d = wq.shape[0]
    return pl.pallas_call(
        project_kernel,
        in_specs=[SM] + [ANY] * 2 + [VM] * 4,
        out_specs=[VM] * 6,
        scratch_shapes=[
            pltpu.VMEM((ROWS, d), BF),
            pltpu.VMEM((WROWS, HD), BF),
            pltpu.VMEM((WROWS, HD), BF),
            pltpu.VMEM((ROWS, 1024), BF),
            pltpu.VMEM((2, 1024), F32),
            pltpu.SemaphoreType.DMA((8,)),
        ],
        out_shape=[
            jax.ShapeDtypeStruct((ROWS, HD), BF),
            jax.ShapeDtypeStruct((ROWS, HD), BF),
        ] + [jax.ShapeDtypeStruct((2 * PART_ROWS, SLICE), BF)] * 4,
        compiler_params=pltpu.CompilerParams(vmem_limit_bytes=16 << 20),
        cost_estimate=pl.CostEstimate(flops=2 * ROWS * d * 1280, bytes_accessed=d * 1280 * 2, transcendentals=0),
        name="project",
    )(meta, *pieces, wq, wk, wv, context_grad)


def forward_kernel(sel, *refs):
    pay_in, kv_in, refs = refs[:8], refs[8], refs[9:]
    ctx_out, q_all, og_all, scale_out, stat_out, p_hbm = refs[:6]
    slot, kv, p_all, s_even, s_odd, acc, mblk, m_ref, l_ref, sem_in, sem_kv, sem_out = refs[6:]
    blocks = KEYS // BLOCK

    kv_copies = kv_copies_of(kv_in, kv, sem_kv)
    for r in range(4):
        for n in range(8):
            @pl.when(sel[4 + r] == n)
            def _():
                pltpu.make_async_copy(pay_in[n].at[sel[8 + r]], slot.at[r], sem_in.at[r]).start()
    for copy in kv_copies:
        copy.start()
    ctx_out[...] = jnp.zeros_like(ctx_out)
    m_ref[...] = jnp.full_like(m_ref, NEG)
    l_ref[...] = jnp.zeros_like(l_ref)
    acc[...] = jnp.zeros_like(acc)
    for r in range(4):
        pltpu.make_async_copy(pay_in[0].at[0], slot.at[r], sem_in.at[r]).wait()
        for j in range(2):
            rows = slice((r * 2 + j) * HD, (r * 2 + j + 1) * HD)
            cols = slice(j * HD, (j + 1) * HD)
            q_all[rows] = slot[r, :ROWS, cols]
            og_all[rows] = slot[r, PART_ROWS:PART_ROWS + ROWS, cols]

    def scores(b, into):
        keys = pl.ds(pl.multiple_of(b * BLOCK, BLOCK), BLOCK)
        into[...] = dot(kv[keys, :HD], q_all[...], NT)

    def soften(b, scored):
        keys = pl.ds(pl.multiple_of(b * BLOCK, BLOCK), BLOCK)
        s = scored[...]
        old = m_ref[...]
        new = jnp.maximum(old, jnp.max(s, axis=0, keepdims=True))
        p = jnp.exp2((s - new) * EXP2_SCALE)
        factor = jnp.exp2((old - new) * EXP2_SCALE)
        l_ref[...] = l_ref[...] * factor + jnp.sum(p, axis=0, keepdims=True)
        pb = p.astype(BF)
        p_all[keys, :] = pb
        pltpu.make_async_copy(p_all.at[keys], p_hbm.at[keys], sem_out.at[b]).start()
        acc[...] = acc[...] * factor + dot(kv[keys, HD:].T, pb, NN)
        m_ref[...] = new
        mblk[pl.ds(b, 1), :] = new

    kv_arrived(0, kv_in, kv, sem_kv)
    scores(0, s_even)

    def forward(b, _):
        kv_arrived(2 * b + 1, kv_in, kv, sem_kv)
        scores(2 * b + 1, s_odd)
        soften(2 * b, s_even)

        @pl.when(b < blocks // 2 - 1)
        def _():
            kv_arrived(2 * b + 2, kv_in, kv, sem_kv)
        scores(lax.rem(2 * b + 2, blocks), s_even)
        soften(2 * b + 1, s_odd)
        return 0

    lax.fori_loop(0, blocks // 2, forward, 0)

    for r in range(4):
        rs = slice(r * SLICE, (r + 1) * SLICE)
        lse0, corr0 = read_stats(slot[r, ROWS:PART_ROWS])
        lse = m_ref[:, rs] * SCALE + jnp.log(l_ref[:, rs])
        top = jnp.maximum(lse, lse0)
        log_norm = top + jnp.log(jnp.exp(lse - top) + jnp.exp(lse0 - top))
        inv = jnp.exp(lse - log_norm) / l_ref[:, rs]
        ctx = acc[:, rs] * inv
        ogt = og_all[rs].astype(F32).T
        corr = jnp.sum(ogt * ctx, axis=0, keepdims=True) + corr0 * jnp.exp(lse0 - log_norm)
        ctx_rows = ctx.T
        for j in range(2):
            ctx_out[sel[20 + r], :, j * HD:(j + 1) * HD] = ctx_rows[j * HD:(j + 1) * HD].astype(BF)
        stat_out[0:1, rs] = log_norm
        stat_out[1:2, rs] = corr
        scale_out[:, rs] = jnp.exp2((mblk[:, rs] - m_ref[:, rs]) * EXP2_SCALE) * inv
    for b in range(blocks):
        keys = pl.ds(b * BLOCK, BLOCK)
        pltpu.make_async_copy(p_all.at[keys], p_hbm.at[keys], sem_out.at[b]).wait()


def kv_copies_of(kv_in, kv, sem):
    blocks = [pl.ds(n * BLOCK, BLOCK) for n in range(KEYS // BLOCK)]
    return [pltpu.make_async_copy(kv_in.at[rows], kv.at[rows], sem.at[n]) for n, rows in enumerate(blocks)]


def kv_arrived(b, kv_in, kv, sem):
    keys = pl.ds(pl.multiple_of(b * BLOCK, BLOCK), BLOCK)
    pltpu.make_async_copy(kv_in.at[keys], kv.at[keys], sem.at[b]).wait()


def backward_kernel(sel, q_all, og_all, factors, stats, p_hbm, *refs):
    kv_in, refs = refs[0], refs[1:]
    dq_out, (dkv_out, kv, dkv, p_all, dqt, held, sem_kv, sem_p, sem_out) = refs[:4], refs[4:]
    blocks = KEYS // WIDE
    for b in range(blocks):
        keys = pl.ds(b * WIDE, WIDE)
        pltpu.make_async_copy(kv_in.at[keys], kv.at[keys], sem_kv.at[b]).start()
        pltpu.make_async_copy(p_hbm.at[keys], p_all.at[keys], sem_p.at[b]).start()
    for out in dq_out:
        out[...] = jnp.zeros_like(out)
    dqt[...] = jnp.zeros_like(dqt)
    corr = stats[1:2]

    def backward(b, _):
        keys = pl.ds(pl.multiple_of(b * WIDE, WIDE), WIDE)
        pltpu.make_async_copy(kv_in.at[keys], kv.at[keys], sem_kv.at[b]).wait()
        dp = dot(kv[keys, HD:], og_all[...], NT)
        pltpu.make_async_copy(p_hbm.at[keys], p_all.at[keys], sem_p.at[b]).wait()
        halves = []
        for h in range(2):
            rows = pl.ds(pl.multiple_of(b * WIDE + h * BLOCK, BLOCK), BLOCK)
            halves.append(p_all[rows, :].astype(F32) * factors[pl.ds(2 * b + h, 1), :])
        a = jnp.concatenate(halves, axis=0)
        ds = (a * (dp - corr)).astype(BF)
        dkv[keys, HD:] = dot(a.astype(BF), og_all[...], NN).astype(BF)
        dkv[keys, :HD] = (dot(ds, q_all[...], NN) * SCALE).astype(BF)
        pltpu.make_async_copy(dkv.at[keys], dkv_out.at[keys], sem_out.at[b]).start()
        dqt[...] += dot(kv[keys, :HD].T, ds, NN)
        return 0

    lax.fori_loop(0, blocks, backward, 0)
    for r in range(4):
        rs = slice(r * SLICE, (r + 1) * SLICE)
        rows = (dqt[:, rs] * SCALE).T
        for j in range(2):
            held[r, :ROWS, j * HD:(j + 1) * HD] = rows[j * HD:(j + 1) * HD].astype(BF)
        held[r, ROWS:] = stat_rows(stats[0:1, rs], stats[1:2, rs])
        for n in range(4):
            @pl.when(sel[12 + r] == n)
            def _():
                dq_out[n][sel[16 + r]] = held[r]
    for b in range(blocks):
        keys = pl.ds(b * WIDE, WIDE)
        pltpu.make_async_copy(dkv.at[keys], dkv_out.at[keys], sem_out.at[b]).wait()


def forward(sel, parts, kv):
    blocks = KEYS // BLOCK
    return pl.pallas_call(
        forward_kernel,
        in_specs=[SM] + [ANY] * 9,
        out_specs=[VM] * 5 + [ANY],
        out_shape=[
            jax.ShapeDtypeStruct((16, ROWS, SLICE), BF),
            jax.ShapeDtypeStruct((WROWS, HD), BF),
            jax.ShapeDtypeStruct((WROWS, HD), BF),
            jax.ShapeDtypeStruct((blocks, WROWS), F32),
            jax.ShapeDtypeStruct((2, WROWS), F32),
            jax.ShapeDtypeStruct((KEYS, WROWS), BF),
        ],
        scratch_shapes=[
            pltpu.VMEM((4, 2 * PART_ROWS, SLICE), BF),
            pltpu.VMEM((KEYS, SLICE), BF),
            pltpu.VMEM((KEYS, WROWS), BF),
            pltpu.VMEM((BLOCK, WROWS), F32),
            pltpu.VMEM((BLOCK, WROWS), F32),
            pltpu.VMEM((HD, WROWS), F32),
            pltpu.VMEM((blocks, WROWS), F32),
            pltpu.VMEM((1, WROWS), F32),
            pltpu.VMEM((1, WROWS), F32),
            pltpu.SemaphoreType.DMA((4,)),
            pltpu.SemaphoreType.DMA((blocks,)),
            pltpu.SemaphoreType.DMA((blocks,)),
        ],
        compiler_params=pltpu.CompilerParams(vmem_limit_bytes=58 << 20),
        cost_estimate=pl.CostEstimate(flops=4 * WROWS * KEYS * HD, bytes_accessed=22 << 20, transcendentals=WROWS * KEYS),
        name="attention_forward",
    )(sel, *parts, kv)


def backward(sel, q_all, og_all, factors, stats, p, kv):
    blocks = KEYS // WIDE
    return pl.pallas_call(
        backward_kernel,
        in_specs=[SM] + [VM] * 4 + [ANY] * 2,
        out_specs=[VM] * 4 + [ANY],
        out_shape=[
            jax.ShapeDtypeStruct((4, PART_ROWS, SLICE), BF),
            jax.ShapeDtypeStruct((4, PART_ROWS, SLICE), BF),
            jax.ShapeDtypeStruct((4, PART_ROWS, SLICE), BF),
            jax.ShapeDtypeStruct((4, PART_ROWS, SLICE), BF),
            jax.ShapeDtypeStruct((KEYS, SLICE), BF),
        ],
        scratch_shapes=[
            pltpu.VMEM((KEYS, SLICE), BF),
            pltpu.VMEM((KEYS, SLICE), BF),
            pltpu.VMEM((KEYS, WROWS), BF),
            pltpu.VMEM((HD, WROWS), F32),
            pltpu.VMEM((4, PART_ROWS, SLICE), BF),
            pltpu.SemaphoreType.DMA((blocks,)),
            pltpu.SemaphoreType.DMA((blocks,)),
            pltpu.SemaphoreType.DMA((blocks,)),
        ],
        compiler_params=pltpu.CompilerParams(vmem_limit_bytes=58 << 20),
        cost_estimate=pl.CostEstimate(flops=8 * WROWS * KEYS * HD, bytes_accessed=24 << 20, transcendentals=0),
        name="attention_backward",
    )(sel, q_all, og_all, factors, stats, p, kv)


def hidden_kernel(meta, *refs):
    dq_in, pay, (k, v, wq, wk, wv, out) = refs[:4], refs[4:8], refs[8:14]
    q_all, og_all, stat_s, own_s, dq_s, dk_s, dv_s, part = refs[14:]
    stack_turned(meta[1], pay, q_all, 0)
    stack_turned(meta[1], pay, og_all, PART_ROWS)
    for n in range(4):
        cols = pl.ds(pl.multiple_of(((meta[1] - n) & 3) * SLICE, SLICE), SLICE)
        stat_s[0:1, cols], stat_s[1:2, cols] = read_stats(dq_in[n][ROWS:])
    mask = wide_mask(meta)
    s = dot(k[...], q_all[...], NT) * SCALE
    dp = dot(v[...], og_all[...], NT)
    a = jnp.where(mask, jnp.exp(jnp.where(mask, s - stat_s[0:1], 0.0)), 0.0)
    ds = (a * (dp - stat_s[1:2])).astype(BF)
    dk_s[...] = (dot(ds, q_all[...], NN) * SCALE).astype(BF)
    dv_s[...] = dot(a.astype(BF), og_all[...], NN).astype(BF)
    for h in range(8):
        own_s[:, h * HD:(h + 1) * HD] = dot(ds[:, h * HD:(h + 1) * HD], k[...], TN) * SCALE
    for n in range(4):
        cols = pl.ds(pl.multiple_of(((meta[1] - n) & 3) * SLICE, SLICE), SLICE)
        dq_s[:, cols] = (dq_in[n][:ROWS].astype(F32) + own_s[:, cols]).astype(BF)
    size = part.shape[1]
    z, c = meta[2], meta[3]
    for n in range(PARTS):
        at = slice(n * size, (n + 1) * size)
        part[...] = dot(dq_s[...], wq[at], NT) + dot(dk_s[...], wk[at], NT) + dot(dv_s[...], wv[at], NT)
        for rc in range(2):
            for dz in range(4):
                start = pl.multiple_of((((z + dz) & 3) * 2 + (c ^ rc)) * 16, 16)
                out[rc, dz, :, at] = part[pl.ds(start, 16), :].astype(BF)


def hidden_grad_parts(meta, dq, pay, k, v, wq, wk, wv):
    d = wq.shape[0]
    return pl.pallas_call(
        hidden_kernel,
        in_specs=[SM] + [VM] * 13,
        out_specs=VM,
        scratch_shapes=[
            pltpu.VMEM((WROWS, HD), BF),
            pltpu.VMEM((WROWS, HD), BF),
            pltpu.VMEM((2, 1024), F32),
            pltpu.VMEM((ROWS, 1024), F32),
            pltpu.VMEM((ROWS, 1024), BF),
            pltpu.VMEM((ROWS, HD), BF),
            pltpu.VMEM((ROWS, HD), BF),
            pltpu.VMEM((ROWS, d // PARTS), F32),
        ],
        out_shape=jax.ShapeDtypeStruct((2, 4, 16, d), BF),
        compiler_params=pltpu.CompilerParams(vmem_limit_bytes=16 << 20),
        cost_estimate=pl.CostEstimate(flops=2 * ROWS * d * 1280, bytes_accessed=d * 1280 * 2, transcendentals=0),
        name="hidden_grad",
    )(meta, *dq, *pay, k, v, wq, wk, wv)


def context_kernel(meta, *refs):
    ctx, pay, dq, (k, v, out, q_all, stat_s, own_s) = refs[:4], refs[4:8], refs[8:12], refs[12:]
    stack_turned(meta[1], pay, q_all, 0)
    for n in range(4):
        cols = pl.ds(pl.multiple_of(((meta[1] - n) & 3) * SLICE, SLICE), SLICE)
        stat_s[0:1, cols], _ = read_stats(dq[n][ROWS:])
    live = live_rows(meta, (ROWS, SLICE))
    mask = wide_mask(meta)
    s = dot(k[...], q_all[...], NT) * SCALE
    a = jnp.where(mask, jnp.exp(jnp.where(mask, s - stat_s[...], 0.0)), 0.0).astype(BF)
    own = [dot(a[:, h * HD:(h + 1) * HD], v[...], TN) for h in range(8)]
    for h in range(8):
        own_s[:, h * HD:(h + 1) * HD] = own[h]
    for n in range(4):
        cols = pl.ds(pl.multiple_of(((meta[1] - n) & 3) * SLICE, SLICE), SLICE)
        out[:, cols] = jnp.where(live, ctx[n][...].astype(F32) + own_s[:, cols], 0.0).astype(BF)


def finish_context(meta, ctx, pay, dq, k, v):
    return pl.pallas_call(
        context_kernel,
        in_specs=[SM] + [VM] * 14,
        out_specs=VM,
        out_shape=jax.ShapeDtypeStruct((ROWS, 1024), BF),
        scratch_shapes=[pltpu.VMEM((WROWS, HD), BF), pltpu.VMEM((1, 1024), F32), pltpu.VMEM((ROWS, 1024), F32)],
        compiler_params=pltpu.CompilerParams(vmem_limit_bytes=16 << 20),
        name="context",
    )(meta, *ctx, *pay, *dq, k, v)


def along_y(parts):
    return [parts[0]] + [move_seq(parts[n], 0, n) for n in (1, 2, 3)]


def add(*terms):
    return sum(t.astype(F32) for t in terms).astype(BF)


def on_device(hidden, wq, wk, wv, prefix_cache, owner_prompt, response_length, context_grad):
    seq, tp = lax.axis_index("seq"), lax.axis_index("tp")
    x, y, z, c = seq // 4, seq % 4, tp // 2, tp % 2
    place = jnp.stack([x, y, z, c]).astype(jnp.int32)
    meta = jnp.concatenate([place, response_length, owner_prompt])

    kv = lax.all_gather(prefix_cache.reshape(CHUNK, SLICE), "seq", axis=0, tiled=True, axis_index_groups=YG)

    passed = [move_tp(hidden, n, 0) for n in (1, 2, 3)]
    group = group_rows([hidden] + passed)
    near = bring_near((wq, wk, wv), (group,))
    k, v, *pay = project(meta, [group, move_tp(group, 0, 1)], *near, context_grad)
    here = along_y(pay)
    parts = ring_gather(jnp.stack(here[:2]), jnp.stack(here[2:]), lambda v, d: move_seq(v, d, 0))

    prompts = jnp.concatenate([part[:, PART_ROWS + ROWS, 0] for part in parts]).astype(jnp.int32)
    spots = jnp.arange(16, dtype=jnp.int32)
    match = prompts == x
    rank = jnp.sum(match[None, :] & (spots[None, :] < spots[:, None]), axis=1)
    chosen = match[None, :] & (rank[None, :] == jnp.arange(4)[:, None])
    spot = jnp.sum(jnp.where(chosen, spots[None, :], 0), axis=1)
    ring_at = spot // 4
    back_x, back_y = -(ring_at ^ (ring_at // 2)) % 4, -spot % 4
    sel_x = (x + back_x) % 4
    sel = jnp.concatenate([spot, spot // 2, spot % 2, back_x, back_y, sel_x * 4 + back_y]).astype(jnp.int32)

    ctx_dense, q_all, og_all, factors, stats, weights = forward(sel, parts, kv)
    ctx_row = lax.psum_scatter(ctx_dense.reshape(-1, SLICE), "seq", scatter_dimension=0, tiled=True, axis_index_groups=XG)
    ctx_row = ctx_row.reshape(4, ROWS, SLICE)
    *dq, dkv = backward(sel, q_all, og_all, factors, stats, weights, kv)
    prefix_grad = lax.psum_scatter(dkv, "seq", scatter_dimension=0, tiled=True, axis_index_groups=YG)
    prefix_grad = prefix_grad.reshape(CHUNK, 1, 2, HD)
    dq = [dq[0]] + [move_seq(dq[n], n, 0) for n in (1, 2, 3)]
    dq = along_y([add(*[part[n] for part in dq]) for n in range(4)])

    parts = hidden_grad_parts(meta, dq, pay, k, v, *bring_near((wq, wk, wv), (dkv,)))
    pair = add(parts[0], move_tp(parts[1], 0, 1))
    hidden_grad = add(pair[0], *[move_tp(pair[n], n, 0) for n in (1, 2, 3)])

    context = finish_context(meta, along_y([ctx_row[n] for n in range(4)]), pay, dq, k, v)
    return context, hidden_grad, prefix_grad


def solution(mesh):
    return jax.shard_map(
        on_device,
        mesh=mesh,
        in_specs=(
            P(("seq", "tp"), None),
            P(None, "tp"),
            P(None, "tp"),
            P(None, "tp"),
            P("seq", "tp", None, None),
            P("seq"),
            P("seq"),
            P("seq", "tp"),
        ),
        out_specs=(P("seq", "tp"), P(("seq", "tp"), None), P("seq", "tp", None, None)),
        check_vma=False,
    )
```

```python
import functools
import math

import jax
import jax.numpy as jnp
from jax import lax
from jax.experimental import pallas as pl
from jax.experimental.pallas import tpu as pltpu
from jax.sharding import PartitionSpec as P

HD = 128
RESP_LEN = 32
ROWS = 128
SLICE = 256
STAT_ROWS = 16
PART_ROWS = ROWS + STAT_ROWS
PAY_ROWS = PART_ROWS + ROWS
CHUNK = 2048
HALF = 1024
PARTS = 5
KEYS = 8192
WROWS = 1024
BLOCK = 1024
WIDE = 2048
SCALE = HD ** -0.5
EXP2_SCALE = SCALE * math.log2(math.e)
NEG = -1.0e30
BF = jnp.bfloat16
F32 = jnp.float32
NT = (((1,), (1,)), ((), ()))
NN = (((1,), (0,)), ((), ()))
TN = (((0,), (0,)), ((), ()))
ANY = pl.BlockSpec(memory_space=pl.ANY)
VM = pl.BlockSpec(memory_space=pltpu.VMEM)
SM = pl.BlockSpec(memory_space=pltpu.SMEM)
XG = [[a * 4 + b for a in range(4)] for b in range(4)]
YG = [[a * 4 + b for b in range(4)] for a in range(4)]


def dot(a, b, dims):
    return lax.dot_general(a, b, dims, preferred_element_type=F32)


def move_tp(x, dz, dc):
    pairs = [(z * 2 + c, ((z + dz) % 4) * 2 + (c + dc) % 2) for z in range(4) for c in range(2)]
    return lax.ppermute(x, "tp", pairs)


def move_seq(x, dx, dy):
    pairs = [(a * 4 + b, ((a + dx) % 4) * 4 + (b + dy) % 4) for a in range(4) for b in range(4)]
    return lax.ppermute(x, "seq", pairs)


def ring_gather(a, b, move):
    pa, nb = move(a, 1), move(b, -1)
    pb, na = move(b, 1), move(a, -1)
    return [a, b, pa, pb, na, nb, move(pa, 1), move(nb, -1)]


def split3(v):
    hi = v.astype(BF).astype(F32)
    mid = (v - hi).astype(BF).astype(F32)
    return hi, mid, v - hi - mid


def stat_rows(first, second, prompt=0):
    rows = list(split3(first)) + list(split3(second))
    tail = jnp.full((STAT_ROWS - 6, SLICE), prompt, jnp.int32).astype(F32)
    return jnp.concatenate(rows + [tail], axis=0).astype(BF)


def read_stats(rows):
    r = rows.astype(F32)
    return r[0:1] + r[1:2] + r[2:3], r[3:4] + r[4:5] + r[5:6]


def causal_mask(lens):
    key = lax.broadcasted_iota(jnp.int32, (ROWS, ROWS), 0)
    row = lax.broadcasted_iota(jnp.int32, (ROWS, ROWS), 1)
    member = lax.shift_right_logical(key, 5)
    length = jnp.where(member == 0, lens[0], jnp.where(member == 1, lens[1], jnp.where(member == 2, lens[2], lens[3])))
    live = (key & (RESP_LEN - 1)) < length
    return (member == lax.shift_right_logical(row, 5)) & (key <= row) & live


def wide_mask(meta):
    return jnp.concatenate([causal_mask([meta[4], meta[5], meta[6], meta[7]])] * 8, axis=1)


def stack_turned(y, slices, into, first):
    for n in range(4):
        for j in range(2):
            start = pl.multiple_of((((y + n) & 3) * 2 + j) * HD, HD)
            into[pl.ds(start, HD)] = slices[n][first:first + ROWS, j * HD:(j + 1) * HD]


def live_rows(meta, shape):
    row = lax.broadcasted_iota(jnp.int32, shape, 0)
    member = lax.shift_right_logical(row, 5)
    length = jnp.where(member == 0, meta[4], jnp.where(member == 1, meta[5], jnp.where(member == 2, meta[6], meta[7])))
    return (row & (RESP_LEN - 1)) < length


def group_kernel(a, b, c, d, after, out):
    for n, piece in enumerate((a, b, c, d)):
        out[n * 16:(n + 1) * 16] = piece[...]


def group_rows(pieces, after):
    return pl.pallas_call(
        group_kernel,
        in_specs=[VM] * 4 + [ANY],
        out_specs=VM,
        out_shape=jax.ShapeDtypeStruct((64, pieces[0].shape[1]), BF),
        compiler_params=pltpu.CompilerParams(vmem_limit_bytes=6 << 20),
        name="group_rows",
    )(*pieces, after)


def near_kernel(*refs):
    ins, outs, sem = refs[:3], refs[-4:-1], refs[-1]
    copies = [pltpu.make_async_copy(src, dst, sem.at[n]) for n, (src, dst) in enumerate(zip(ins, outs))]
    for copy in copies:
        copy.start()
    for copy in copies:
        copy.wait()


def bring_near(weights, after=()):
    d = weights[0].shape[0]
    return pl.pallas_call(
        near_kernel,
        in_specs=[ANY] * (3 + len(after)),
        out_specs=[VM] * 3,
        out_shape=[pltpu.VMEM(w.shape, BF) for w in weights],
        scratch_shapes=[pltpu.SemaphoreType.DMA((3,))],
        compiler_params=pltpu.CompilerParams(vmem_limit_bytes=4 << 20),
        cost_estimate=pl.CostEstimate(flops=0, bytes_accessed=d * 2560, transcendentals=0),
        name="bring_near",
    )(*weights, *after)


def project_kernel(meta, *refs):
    pieces, (wq_s, wk_s, wv_s), cg = refs[:2], refs[2:5], refs[5]
    k_out, v_out, kept, pay = refs[6], refs[7], refs[8], refs[9:13]
    seg, q_all, og_all, q_s, stat_s, sem = refs[13:]
    z, c = meta[2], meta[3]
    copies = []
    for rc in range(2):
        for dz in range(4):
            start = pl.multiple_of((((z - dz) & 3) * 2 + (c ^ rc)) * 16, 16)
            source = pieces[rc].at[pl.ds(dz * 16, 16)]
            copies.append(pltpu.make_async_copy(source, seg.at[pl.ds(start, 16)], sem.at[rc * 4 + dz]))
    for copy in copies:
        copy.start()
    live = live_rows(meta, (ROWS, SLICE))
    for n in range(4):
        start = pl.multiple_of(((meta[1] + n) & 3) * SLICE, SLICE)
        grads = cg[:, pl.ds(start, SLICE)]
        pay[n][PART_ROWS:] = jnp.where(live, grads, jnp.zeros_like(grads))
    stack_turned(meta[1], pay, og_all, PART_ROWS)
    for copy in copies:
        copy.wait()
    k_out[...] = dot(seg[...], wk_s[...], NN).astype(BF)
    v_out[...] = dot(seg[...], wv_s[...], NN).astype(BF)
    q = dot(seg[...], wq_s[...], NN).astype(BF)
    q_s[...] = q
    for h in range(8):
        q_all[h * HD:(h + 1) * HD] = q[:, h * HD:(h + 1) * HD]
    mask = wide_mask(meta)
    s = jnp.where(mask, dot(k_out[...], q_all[...], NT) * SCALE, NEG)
    top = jnp.max(s, axis=0, keepdims=True)
    p = jnp.where(mask, jnp.exp(s - top), 0.0)
    total = jnp.sum(p, axis=0, keepdims=True)
    dp = dot(v_out[...], og_all[...], NT)
    lse = top + jnp.log(total)
    corr = jnp.sum(p.astype(BF).astype(F32) * dp, axis=0, keepdims=True) / total
    stat_s[0:1] = lse
    stat_s[1:2] = corr
    for n in range(4):
        cols = pl.ds(pl.multiple_of(((meta[1] + n) & 3) * SLICE, SLICE), SLICE)
        pay[n][:ROWS] = q_s[:, cols]
        pay[n][ROWS:PART_ROWS] = stat_rows(stat_s[0:1, cols], stat_s[1:2, cols], meta[8])
        kept[n] = pay[n][...]


def project(meta, pieces, wq, wk, wv, context_grad):
    d = wq.shape[0]
    return pl.pallas_call(
        project_kernel,
        in_specs=[SM] + [ANY] * 2 + [VM] * 4,
        out_specs=[VM] * 7,
        scratch_shapes=[
            pltpu.VMEM((ROWS, d), BF),
            pltpu.VMEM((WROWS, HD), BF),
            pltpu.VMEM((WROWS, HD), BF),
            pltpu.VMEM((ROWS, 1024), BF),
            pltpu.VMEM((2, 1024), F32),
            pltpu.SemaphoreType.DMA((8,)),
        ],
        out_shape=[
            jax.ShapeDtypeStruct((ROWS, HD), BF),
            jax.ShapeDtypeStruct((ROWS, HD), BF),
            jax.ShapeDtypeStruct((4, PAY_ROWS, SLICE), BF),
        ] + [jax.ShapeDtypeStruct((PAY_ROWS, SLICE), BF)] * 4,
        compiler_params=pltpu.CompilerParams(vmem_limit_bytes=16 << 20),
        cost_estimate=pl.CostEstimate(flops=2 * ROWS * d * 1280, bytes_accessed=d * 1280 * 2, transcendentals=0),
        name="project",
    )(meta, *pieces, wq, wk, wv, context_grad)


def forward_kernel(sel, *refs):
    pay_in, kv_in, refs = refs[:8], refs[8], refs[9:]
    ctx_out, q_all, og_all, scale_out, stat_out, p_hbm = refs[:6]
    slot, kv, p_all, s_even, s_odd, acc, mblk, m_ref, l_ref, sem_in, sem_kv, sem_out = refs[6:]
    blocks = KEYS // BLOCK

    kv_copies = kv_copies_of(kv_in, kv, sem_kv)
    for r in range(4):
        for n in range(8):
            @pl.when(sel[4 + r] == n)
            def _():
                pltpu.make_async_copy(pay_in[n].at[sel[8 + r]], slot.at[r], sem_in.at[r]).start()
    for copy in kv_copies:
        copy.start()
    ctx_out[...] = jnp.zeros_like(ctx_out)
    m_ref[...] = jnp.full_like(m_ref, NEG)
    l_ref[...] = jnp.zeros_like(l_ref)
    acc[...] = jnp.zeros_like(acc)
    for r in range(4):
        pltpu.make_async_copy(pay_in[0].at[0], slot.at[r], sem_in.at[r]).wait()
        for j in range(2):
            rows = slice((r * 2 + j) * HD, (r * 2 + j + 1) * HD)
            cols = slice(j * HD, (j + 1) * HD)
            q_all[rows] = slot[r, :ROWS, cols]
            og_all[rows] = slot[r, PART_ROWS:PART_ROWS + ROWS, cols]

    def scores(b, into):
        keys = pl.ds(pl.multiple_of(b * BLOCK, BLOCK), BLOCK)
        into[...] = dot(kv[keys, :HD], q_all[...], NT)

    def soften(b, scored):
        keys = pl.ds(pl.multiple_of(b * BLOCK, BLOCK), BLOCK)
        s = scored[...]
        old = m_ref[...]
        new = jnp.maximum(old, jnp.max(s, axis=0, keepdims=True))
        p = jnp.exp2((s - new) * EXP2_SCALE)
        factor = jnp.exp2((old - new) * EXP2_SCALE)
        l_ref[...] = l_ref[...] * factor + jnp.sum(p, axis=0, keepdims=True)
        pb = p.astype(BF)
        p_all[keys, :] = pb
        pltpu.make_async_copy(p_all.at[keys], p_hbm.at[keys], sem_out.at[b]).start()
        acc[...] = acc[...] * factor + dot(kv[keys, HD:].T, pb, NN)
        m_ref[...] = new
        mblk[pl.ds(b, 1), :] = new

    kv_arrived(0, kv_in, kv, sem_kv)
    scores(0, s_even)

    def forward(b, _):
        kv_arrived(2 * b + 1, kv_in, kv, sem_kv)
        scores(2 * b + 1, s_odd)
        soften(2 * b, s_even)

        @pl.when(b < blocks // 2 - 1)
        def _():
            kv_arrived(2 * b + 2, kv_in, kv, sem_kv)
        scores(lax.rem(2 * b + 2, blocks), s_even)
        soften(2 * b + 1, s_odd)
        return 0

    lax.fori_loop(0, blocks // 2, forward, 0)

    for r in range(4):
        rs = slice(r * SLICE, (r + 1) * SLICE)
        lse0, corr0 = read_stats(slot[r, ROWS:PART_ROWS])
        lse = m_ref[:, rs] * SCALE + jnp.log(l_ref[:, rs])
        top = jnp.maximum(lse, lse0)
        log_norm = top + jnp.log(jnp.exp(lse - top) + jnp.exp(lse0 - top))
        inv = jnp.exp(lse - log_norm) / l_ref[:, rs]
        ctx = acc[:, rs] * inv
        ogt = og_all[rs].astype(F32).T
        corr = jnp.sum(ogt * ctx, axis=0, keepdims=True) + corr0 * jnp.exp(lse0 - log_norm)
        ctx_rows = ctx.T
        for j in range(2):
            ctx_out[sel[20 + r], :, j * HD:(j + 1) * HD] = ctx_rows[j * HD:(j + 1) * HD].astype(BF)
        stat_out[0:1, rs] = log_norm
        stat_out[1:2, rs] = corr
        scale_out[:, rs] = jnp.exp2((mblk[:, rs] - m_ref[:, rs]) * EXP2_SCALE) * inv
    for b in range(blocks):
        keys = pl.ds(b * BLOCK, BLOCK)
        pltpu.make_async_copy(p_all.at[keys], p_hbm.at[keys], sem_out.at[b]).wait()


def kv_copies_of(kv_in, kv, sem):
    blocks = [pl.ds(n * BLOCK, BLOCK) for n in range(KEYS // BLOCK)]
    return [pltpu.make_async_copy(kv_in.at[rows], kv.at[rows], sem.at[n]) for n, rows in enumerate(blocks)]


def kv_arrived(b, kv_in, kv, sem):
    keys = pl.ds(pl.multiple_of(b * BLOCK, BLOCK), BLOCK)
    pltpu.make_async_copy(kv_in.at[keys], kv.at[keys], sem.at[b]).wait()


def backward_kernel(sel, q_all, og_all, factors, stats, p_hbm, *refs):
    kv_in, refs = refs[0], refs[1:]
    dq_out, (dkv_out, kv, dkv, p_all, dqt, held, sem_kv, sem_p, sem_out) = refs[:4], refs[4:]
    blocks = KEYS // WIDE
    for b in range(blocks):
        keys = pl.ds(b * WIDE, WIDE)
        pltpu.make_async_copy(kv_in.at[keys], kv.at[keys], sem_kv.at[b]).start()
        pltpu.make_async_copy(p_hbm.at[keys], p_all.at[keys], sem_p.at[b]).start()
    for out in dq_out:
        out[...] = jnp.zeros_like(out)
    dqt[...] = jnp.zeros_like(dqt)
    corr = stats[1:2]

    def backward(b, _):
        keys = pl.ds(pl.multiple_of(b * WIDE, WIDE), WIDE)
        pltpu.make_async_copy(kv_in.at[keys], kv.at[keys], sem_kv.at[b]).wait()
        dp = dot(kv[keys, HD:], og_all[...], NT)
        pltpu.make_async_copy(p_hbm.at[keys], p_all.at[keys], sem_p.at[b]).wait()
        halves = []
        for h in range(2):
            rows = pl.ds(pl.multiple_of(b * WIDE + h * BLOCK, BLOCK), BLOCK)
            halves.append(p_all[rows, :].astype(F32) * factors[pl.ds(2 * b + h, 1), :])
        a = jnp.concatenate(halves, axis=0)
        ds = (a * (dp - corr)).astype(BF)
        dkv[keys, HD:] = dot(a.astype(BF), og_all[...], NN).astype(BF)
        dkv[keys, :HD] = (dot(ds, q_all[...], NN) * SCALE).astype(BF)
        pltpu.make_async_copy(dkv.at[keys], dkv_out.at[keys], sem_out.at[b]).start()
        dqt[...] += dot(kv[keys, :HD].T, ds, NN)
        return 0

    lax.fori_loop(0, blocks, backward, 0)
    for r in range(4):
        rs = slice(r * SLICE, (r + 1) * SLICE)
        rows = (dqt[:, rs] * SCALE).T
        for j in range(2):
            held[r, :ROWS, j * HD:(j + 1) * HD] = rows[j * HD:(j + 1) * HD].astype(BF)
        held[r, ROWS:] = stat_rows(stats[0:1, rs], stats[1:2, rs])
        for n in range(4):
            @pl.when(sel[12 + r] == n)
            def _():
                dq_out[n][sel[16 + r]] = held[r]
    for b in range(blocks):
        keys = pl.ds(b * WIDE, WIDE)
        pltpu.make_async_copy(dkv.at[keys], dkv_out.at[keys], sem_out.at[b]).wait()


def forward(sel, parts, kv):
    blocks = KEYS // BLOCK
    return pl.pallas_call(
        forward_kernel,
        in_specs=[SM] + [ANY] * 9,
        out_specs=[VM] * 5 + [ANY],
        out_shape=[
            jax.ShapeDtypeStruct((16, ROWS, SLICE), BF),
            jax.ShapeDtypeStruct((WROWS, HD), BF),
            jax.ShapeDtypeStruct((WROWS, HD), BF),
            jax.ShapeDtypeStruct((blocks, WROWS), F32),
            jax.ShapeDtypeStruct((2, WROWS), F32),
            jax.ShapeDtypeStruct((KEYS, WROWS), BF),
        ],
        scratch_shapes=[
            pltpu.VMEM((4, PAY_ROWS, SLICE), BF),
            pltpu.VMEM((KEYS, SLICE), BF),
            pltpu.VMEM((KEYS, WROWS), BF),
            pltpu.VMEM((BLOCK, WROWS), F32),
            pltpu.VMEM((BLOCK, WROWS), F32),
            pltpu.VMEM((HD, WROWS), F32),
            pltpu.VMEM((blocks, WROWS), F32),
            pltpu.VMEM((1, WROWS), F32),
            pltpu.VMEM((1, WROWS), F32),
            pltpu.SemaphoreType.DMA((4,)),
            pltpu.SemaphoreType.DMA((blocks,)),
            pltpu.SemaphoreType.DMA((blocks,)),
        ],
        compiler_params=pltpu.CompilerParams(vmem_limit_bytes=58 << 20),
        cost_estimate=pl.CostEstimate(flops=4 * WROWS * KEYS * HD, bytes_accessed=22 << 20, transcendentals=WROWS * KEYS),
        name="attention_forward",
    )(sel, *parts, kv)


def backward(sel, q_all, og_all, factors, stats, p, kv):
    blocks = KEYS // WIDE
    return pl.pallas_call(
        backward_kernel,
        in_specs=[SM] + [VM] * 4 + [ANY] * 2,
        out_specs=[VM] * 4 + [ANY],
        out_shape=[
            jax.ShapeDtypeStruct((4, PART_ROWS, SLICE), BF),
            jax.ShapeDtypeStruct((4, PART_ROWS, SLICE), BF),
            jax.ShapeDtypeStruct((4, PART_ROWS, SLICE), BF),
            jax.ShapeDtypeStruct((4, PART_ROWS, SLICE), BF),
            jax.ShapeDtypeStruct((KEYS, SLICE), BF),
        ],
        scratch_shapes=[
            pltpu.VMEM((KEYS, SLICE), BF),
            pltpu.VMEM((KEYS, SLICE), BF),
            pltpu.VMEM((KEYS, WROWS), BF),
            pltpu.VMEM((HD, WROWS), F32),
            pltpu.VMEM((4, PART_ROWS, SLICE), BF),
            pltpu.SemaphoreType.DMA((blocks,)),
            pltpu.SemaphoreType.DMA((blocks,)),
            pltpu.SemaphoreType.DMA((blocks,)),
        ],
        compiler_params=pltpu.CompilerParams(vmem_limit_bytes=58 << 20),
        cost_estimate=pl.CostEstimate(flops=8 * WROWS * KEYS * HD, bytes_accessed=24 << 20, transcendentals=0),
        name="attention_backward",
    )(sel, q_all, og_all, factors, stats, p, kv)


def hidden_kernel(meta, *refs):
    dq_in, kept, (k, v, wq, wk, wv, out) = refs[:4], refs[4], refs[5:11]
    q_all, og_all, stat_s, own_s, dq_s, dk_s, dv_s, part = refs[11:]
    pay = [kept.at[n] for n in range(4)]
    stack_turned(meta[1], pay, q_all, 0)
    stack_turned(meta[1], pay, og_all, PART_ROWS)
    for n in range(4):
        cols = pl.ds(pl.multiple_of(((meta[1] - n) & 3) * SLICE, SLICE), SLICE)
        stat_s[0:1, cols], stat_s[1:2, cols] = read_stats(dq_in[n][ROWS:])
    mask = wide_mask(meta)
    s = dot(k[...], q_all[...], NT) * SCALE
    dp = dot(v[...], og_all[...], NT)
    a = jnp.where(mask, jnp.exp(jnp.where(mask, s - stat_s[0:1], 0.0)), 0.0)
    ds = (a * (dp - stat_s[1:2])).astype(BF)
    dk_s[...] = (dot(ds, q_all[...], NN) * SCALE).astype(BF)
    dv_s[...] = dot(a.astype(BF), og_all[...], NN).astype(BF)
    for h in range(8):
        own_s[:, h * HD:(h + 1) * HD] = dot(ds[:, h * HD:(h + 1) * HD], k[...], TN) * SCALE
    for n in range(4):
        cols = pl.ds(pl.multiple_of(((meta[1] - n) & 3) * SLICE, SLICE), SLICE)
        dq_s[:, cols] = (dq_in[n][:ROWS].astype(F32) + own_s[:, cols]).astype(BF)
    size = part.shape[1]
    z, c = meta[2], meta[3]
    for n in range(PARTS):
        at = slice(n * size, (n + 1) * size)
        part[...] = dot(dq_s[...], wq[at], NT) + dot(dk_s[...], wk[at], NT) + dot(dv_s[...], wv[at], NT)
        for rc in range(2):
            for dz in range(4):
                start = pl.multiple_of((((z + dz) & 3) * 2 + (c ^ rc)) * 16, 16)
                out[rc, dz, :, at] = part[pl.ds(start, 16), :].astype(BF)


def hidden_grad_parts(meta, dq, pay, k, v, wq, wk, wv):
    d = wq.shape[0]
    return pl.pallas_call(
        hidden_kernel,
        in_specs=[SM] + [VM] * 10,
        out_specs=VM,
        scratch_shapes=[
            pltpu.VMEM((WROWS, HD), BF),
            pltpu.VMEM((WROWS, HD), BF),
            pltpu.VMEM((2, 1024), F32),
            pltpu.VMEM((ROWS, 1024), F32),
            pltpu.VMEM((ROWS, 1024), BF),
            pltpu.VMEM((ROWS, HD), BF),
            pltpu.VMEM((ROWS, HD), BF),
            pltpu.VMEM((ROWS, d // PARTS), F32),
        ],
        out_shape=jax.ShapeDtypeStruct((2, 4, 16, d), BF),
        compiler_params=pltpu.CompilerParams(vmem_limit_bytes=16 << 20),
        cost_estimate=pl.CostEstimate(flops=2 * ROWS * d * 1280, bytes_accessed=d * 1280 * 2, transcendentals=0),
        name="hidden_grad",
    )(meta, *dq, pay, k, v, wq, wk, wv)


def context_kernel(meta, *refs):
    ctx, kept, dq, (k, v, out, q_all, stat_s, own_s) = refs[:4], refs[4], refs[5:9], refs[9:]
    stack_turned(meta[1], [kept.at[n] for n in range(4)], q_all, 0)
    for n in range(4):
        cols = pl.ds(pl.multiple_of(((meta[1] - n) & 3) * SLICE, SLICE), SLICE)
        stat_s[0:1, cols], _ = read_stats(dq[n][ROWS:])
    live = live_rows(meta, (ROWS, SLICE))
    mask = wide_mask(meta)
    s = dot(k[...], q_all[...], NT) * SCALE
    a = jnp.where(mask, jnp.exp(jnp.where(mask, s - stat_s[...], 0.0)), 0.0).astype(BF)
    own = [dot(a[:, h * HD:(h + 1) * HD], v[...], TN) for h in range(8)]
    for h in range(8):
        own_s[:, h * HD:(h + 1) * HD] = own[h]
    for n in range(4):
        cols = pl.ds(pl.multiple_of(((meta[1] - n) & 3) * SLICE, SLICE), SLICE)
        out[:, cols] = jnp.where(live, ctx[n][...].astype(F32) + own_s[:, cols], 0.0).astype(BF)


def finish_context(meta, ctx, pay, dq, k, v):
    return pl.pallas_call(
        context_kernel,
        in_specs=[SM] + [VM] * 11,
        out_specs=VM,
        out_shape=jax.ShapeDtypeStruct((ROWS, 1024), BF),
        scratch_shapes=[pltpu.VMEM((WROWS, HD), BF), pltpu.VMEM((1, 1024), F32), pltpu.VMEM((ROWS, 1024), F32)],
        compiler_params=pltpu.CompilerParams(vmem_limit_bytes=16 << 20),
        name="context",
    )(meta, *ctx, pay, *dq, k, v)


def along_y(parts):
    return [parts[0]] + [move_seq(parts[n], 0, n) for n in (1, 2, 3)]


def add(*terms):
    return sum(t.astype(F32) for t in terms).astype(BF)


def on_device(hidden, wq, wk, wv, prefix_cache, owner_prompt, response_length, context_grad):
    seq, tp = lax.axis_index("seq"), lax.axis_index("tp")
    x, y, z, c = seq // 4, seq % 4, tp // 2, tp % 2
    place = jnp.stack([x, y, z, c]).astype(jnp.int32)
    meta = jnp.concatenate([place, response_length, owner_prompt])

    kv = lax.all_gather(prefix_cache.reshape(CHUNK, SLICE), "seq", axis=0, tiled=True, axis_index_groups=YG)

    passed = [move_tp(hidden, n, 0) for n in (1, 2, 3)]
    near = bring_near((wq, wk, wv), (meta,))
    group = group_rows([hidden] + passed, near[1])
    k, v, kept, *pay = project(meta, [group, move_tp(group, 0, 1)], *near, context_grad)
    here = along_y(pay)
    parts = ring_gather(jnp.stack(here[:2]), jnp.stack(here[2:]), lambda v, d: move_seq(v, d, 0))

    prompts = jnp.concatenate([part[:, ROWS + 6, 0] for part in parts]).astype(jnp.int32)
    spots = jnp.arange(16, dtype=jnp.int32)
    match = prompts == x
    rank = jnp.sum(match[None, :] & (spots[None, :] < spots[:, None]), axis=1)
    chosen = match[None, :] & (rank[None, :] == jnp.arange(4)[:, None])
    spot = jnp.sum(jnp.where(chosen, spots[None, :], 0), axis=1)
    ring_at = spot // 4
    back_x, back_y = -(ring_at ^ (ring_at // 2)) % 4, -spot % 4
    sel_x = (x + back_x) % 4
    sel = jnp.concatenate([spot, spot // 2, spot % 2, back_x, back_y, sel_x * 4 + back_y]).astype(jnp.int32)

    ctx_dense, q_all, og_all, factors, stats, weights = forward(sel, parts, kv)
    ctx_row = lax.psum_scatter(ctx_dense.reshape(-1, SLICE), "seq", scatter_dimension=0, tiled=True, axis_index_groups=XG)
    ctx_row = ctx_row.reshape(4, ROWS, SLICE)
    *dq, dkv = backward(sel, q_all, og_all, factors, stats, weights, kv)
    prefix_grad = lax.psum_scatter(dkv, "seq", scatter_dimension=0, tiled=True, axis_index_groups=YG)
    prefix_grad = prefix_grad.reshape(CHUNK, 1, 2, HD)
    dq = [dq[0]] + [move_seq(dq[n], n, 0) for n in (1, 2, 3)]
    dq = along_y([add(*[part[n] for part in dq]) for n in range(4)])

    parts = hidden_grad_parts(meta, dq, kept, k, v, *bring_near((wq, wk, wv), (dkv,)))
    pair = add(parts[0], move_tp(parts[1], 0, 1))
    hidden_grad = add(pair[0], *[move_tp(pair[n], n, 0) for n in (1, 2, 3)])

    context = finish_context(meta, along_y([ctx_row[n] for n in range(4)]), kept, dq, k, v)
    return context, hidden_grad, prefix_grad


def solution(mesh):
    return jax.shard_map(
        on_device,
        mesh=mesh,
        in_specs=(
            P(("seq", "tp"), None),
            P(None, "tp"),
            P(None, "tp"),
            P(None, "tp"),
            P("seq", "tp", None, None),
            P("seq"),
            P("seq"),
            P("seq", "tp"),
        ),
        out_specs=(P("seq", "tp"), P(("seq", "tp"), None), P("seq", "tp", None, None)),
        check_vma=False,
    )
```
